256 devices in a mesh: beam: 8 (over z_hi, core), tile: 32 (over z_lo, x, y).
Axes of the slice: x: 4, y: 4, z: 8 (z_hi: 4, z_lo: 2; z = z_hi * 2 + z_lo), core: 2. Of those that a mesh axis runs over, the one named last changes fastest.
Arguments:
- model_grid: float32 [8, 2, 2048, 2048], P('beam', None, 'tile'), may hold values from -4 to 4
- observed: float32 [8, 2048, 2, 256], P('beam', 'tile'), may hold values from -6 to 6
- coords: float32 [8, 2048, 2, 256], P('beam', 'tile'), may hold values from 8 to 56
- vis_count: int32 [8, 32, 64], P('beam', 'tile'), may hold values from 1 to 256, 10240 in all within a row
- subgrid_block: int32 [8, 32, 64], P('beam', 'tile'), may hold values from 0 to 63, each once within a row
- subgrid_cell: int32 [8, 32, 64], P('beam', 'tile'), may hold values from 0 to 31
- beam_gain: float32 [8, 2048, 2048], P('beam', 'tile'), may hold values from 0.1 to 1
- column_shift: int32 [8], P('beam'), may hold values from 0 to 32
- row_offset: int32 [8], P('beam'), may hold values from 0 to 2048
- interp_index: int32 [8, 2], P('beam'), may hold values from 0 to 7
- interp_taps: float32 [8, 5], replicated, may hold values from 0.05 to 0.5
Outputs:
- gradient_sky: float32 [2, 2048, 4096], P(None, 'tile', 'beam')
The draws below stay inside these ranges and needn't reach their ends.
Inputs may be any that keep to these rules, and one draw needn't show every extreme that they name: `vis_count`: in each slab of each beam the 64 counts sum to 10240 and the largest is 256. `subgrid_block`: each slab's row is a permutation.
All inputs are finite; a program needn't handle non-finite values.
Results may differ from the reference program's by a relative error of at most 0.00013.
Values sent between devices are 32-bit elements; how exact they have to be, the bound alone decides.
A program may use at most 64 MiB of HBM per device.

```python
import math
from functools import reduce
import jax
import jax.numpy as jnp
import numpy as np
from jax import lax

G = 2048
SUBG = 64
NV = 256
SUB_DEV = 64
NPHASE = 8
BEAMS = 8
SUBS = 2048
CELLS_DEV = 32
N_TILE = 32


def touch_ends(result, key, least, largest):
    dims = result.shape
    spot = [jax.random.randint(jax.random.fold_in(key, axis), (), 0, dims[axis]) for axis in range(len(dims))]
    result = result.at[tuple(spot)].set(least)
    longest = dims.index(max(dims))
    spot[longest] = (spot[longest] + 1) % dims[longest]
    return result.at[tuple(spot)].set(largest)


def block_levels(stream_key, shape, shards, low, top_value):
    level = 1.0
    for axis_at, blocks in shards:
        draws = jax.random.uniform(jax.random.fold_in(jax.random.fold_in(stream_key, 6), axis_at), (blocks,), jnp.float32, low / len(shards), top_value / len(shards))
        level = level * jnp.repeat(jnp.exp(draws), shape[axis_at] // blocks).reshape((-1,) + (1,) * (len(shape) - 1 - axis_at))
    return level


def rank_table(amount, skew):
    loads = [(1 << 20) // math.isqrt(standing ** skew) + 1 for standing in range(1, amount + 1)]
    spread = 1 + sum(loads) // (1 << 30)
    return np.cumsum(np.array([max(1, weight // spread) for weight in loads]))


def ranked(own_key, shape, amount, slope):
    grid = rank_table(amount, slope)
    ticket = jax.random.randint(jax.random.fold_in(own_key, 1), shape, 0, int(grid[amount - 1]))
    standing = jnp.searchsorted(jnp.asarray(grid, jnp.int32), ticket, side="right")
    return jax.random.permutation(jax.random.fold_in(own_key, 2), amount)[standing].astype(jnp.int32)


def length_profile(count, total, most, lean):
    weights = [(1 << 20) // math.isqrt(rank ** lean) + 1 for rank in range(2, count + 1)]
    spare, given = total - most - (count - 1), [1] * (count - 1)
    while spare > 0:
        free = [i for i in range(count - 1) if given[i] < most]
        mass, budget = sum([weights[i] for i in free]), spare
        for i in free:
            addition = min(most - given[i], max(1, budget * weights[i] // mass), spare)
            given[i] = given[i] + addition
            spare = spare - addition
    return np.array([most] + given)


def ragged(stream_key, amount, total, reach, slope):
    if amount == 2:
        one = jax.random.randint(stream_key, (), max(1, total - reach), min(reach, total - 1) + 1)
        return jnp.stack([one, total - one])
    sizes = jnp.asarray(length_profile(amount, total, reach, slope), jnp.int32)
    pairs = (amount - 1) // 2
    giver, sink = sizes[1:1 + 2 * pairs:2], sizes[2:2 + 2 * pairs:2]
    room = jnp.minimum(giver - 1, reach - sink)
    moved = jax.random.randint(jax.random.fold_in(stream_key, 1), (pairs,), 0, 1 << 20) % (room + 1)
    sizes = sizes.at[1:1 + 2 * pairs:2].set(giver - moved).at[2:2 + 2 * pairs:2].set(sink + moved)
    return sizes[jax.random.permutation(jax.random.fold_in(stream_key, 2), amount)]


def scatter_about(own_key, shape, deviation, bound, cuts=(), kind=jnp.bfloat16):
    values = jax.random.normal(own_key, shape, jnp.float32) * deviation
    if len(cuts) > 0:
        values = block_levels(own_key, shape, cuts, -0.22, 0.18) * values
    return jnp.clip(values, min=-bound, max=bound).astype(kind)


def setup_inputs(seed: int = 0) -> dict:
    seeds = jax.random.split(jax.random.key(seed), 12)
    return {
        "model_grid": scatter_about(seeds[0], (BEAMS, 2, G, G), 0.5, 4.0, ((0, 8), (2, 32)), jnp.float32),
        "observed": scatter_about(seeds[1], (BEAMS, SUBS, 2, NV), 1.0, 6.0, ((0, 8), (1, 32)), jnp.float32),
        "coords": jnp.clip(8.0 + 48.0 * jax.random.uniform(seeds[2], (BEAMS, SUBS, 2, NV), jnp.float32) ** block_levels(seeds[2], (BEAMS, SUBS, 2, NV), ((0, 8), (1, 32)), -0.2, 0.2), 8.0, 56.0),
        "vis_count": jax.vmap(lambda own: ragged(own, SUB_DEV, SUB_DEV * NV * 5 // 8, NV, 2))(jax.random.split(seeds[3], BEAMS * N_TILE)).reshape((BEAMS, N_TILE, SUB_DEV)).astype(jnp.int32),
        "subgrid_block": jax.vmap(lambda own: jax.random.permutation(own, SUB_DEV))(jax.random.split(seeds[4], BEAMS * N_TILE)).reshape((BEAMS, N_TILE, SUB_DEV)).astype(jnp.int32),
        "subgrid_cell": touch_ends(ranked(seeds[5], (BEAMS, N_TILE, SUB_DEV), CELLS_DEV, 2), jax.random.fold_in(seeds[5], 3), 0, CELLS_DEV - 1).astype(jnp.int32),
        "beam_gain": jnp.clip(jnp.exp(math.log(1.0) - 2.3025851 * jax.random.uniform(seeds[6], (BEAMS, G, G), jnp.float32) ** block_levels(seeds[6], (BEAMS, G, G), ((0, 8), (1, 32)), -0.2, 0.2)), 0.1, 1.0),
        "column_shift": touch_ends(jax.random.randint(seeds[7], (BEAMS,), 0, N_TILE + 1), jax.random.fold_in(seeds[7], 1), 0, N_TILE).astype(jnp.int32),
        "row_offset": touch_ends(jax.random.randint(seeds[8], (BEAMS,), 0, G + 1), jax.random.fold_in(seeds[8], 1), 0, G).astype(jnp.int32),
        "interp_index": touch_ends(jax.random.randint(seeds[9], (BEAMS, 2), 0, NPHASE), jax.random.fold_in(seeds[9], 1), 0, NPHASE - 1).astype(jnp.int32),
        "interp_taps": jnp.clip(jax.random.uniform(seeds[10], (NPHASE, 5), jnp.float32, 0.05, 0.5), 0.05, 0.5),
    }


kernel_scale = 3.0
highest = lax.Precision.HIGHEST


def kernel_rows(position, extent):
    offsets = jnp.arange(extent).astype(position.dtype)
    return jnp.exp(-jnp.abs(offsets - position[..., None]) / kernel_scale)


def residual_grid(model, observed, coords, counts, block_order, cell_ids):
    subgrid_side = SUBG
    cell_rows = G // subgrid_side
    cell_table = model.reshape(2, cell_rows, subgrid_side, cell_rows, subgrid_side).transpose(1, 3, 0, 2, 4).reshape(cell_rows * cell_rows, 2, subgrid_side, subgrid_side)
    windows = cell_table[cell_ids]
    visible = observed[block_order]
    placed = coords[block_order]
    slot_count = observed.shape[-1]
    live_mask = (jnp.arange(slot_count, dtype=jnp.int32)[None, :] < counts[:, None]).astype(model.dtype)
    along_v = kernel_rows(placed[:, 0], subgrid_side)
    along_u = kernel_rows(placed[:, 1], subgrid_side)
    partial_rows = jnp.einsum("snk,sckl->scnl", along_v, windows, precision=highest)
    predicted = jnp.sum(partial_rows * along_u[:, None], axis=-1)
    residual = live_mask[:, None, :] * (visible - predicted)
    weighted = residual[..., None] * along_u[:, None]
    patches = jnp.einsum("snk,scnl->sckl", along_v, weighted, precision=highest)
    summed = jnp.zeros_like(cell_table).at[cell_ids].add(patches)
    return summed.reshape(cell_rows, cell_rows, 2, subgrid_side, subgrid_side).transpose(2, 0, 3, 1, 4).reshape(2, G, G)


def reference(model_grid, observed, coords, vis_count, subgrid_block, subgrid_cell, beam_gain, column_shift, row_offset, interp_index, interp_taps):
    column_width = G // N_TILE
    canvas = jnp.zeros((2 * G, 2 * G), jnp.float32)
    tile_ids = jnp.arange(N_TILE, dtype=jnp.int32)[:, None]
    for beam_number in range(BEAMS):
        block_order = (tile_ids * SUB_DEV + subgrid_block[beam_number]).reshape(-1).astype(jnp.int32)
        cell_ids = (tile_ids * CELLS_DEV + subgrid_cell[beam_number]).reshape(-1).astype(jnp.int32)
        counts = vis_count[beam_number].reshape(-1)
        uv_grid = residual_grid(model_grid[beam_number], observed[beam_number], coords[beam_number], counts, block_order, cell_ids)
        spectrum = uv_grid[0] + 1j * uv_grid[1]
        beam_image = (G * jnp.real(jnp.fft.ifft2(spectrum))).T
        taps_x = interp_taps[interp_index[beam_number, 0]]
        taps_y = interp_taps[interp_index[beam_number, 1]]
        padded = jnp.pad(beam_image, ((2, 2), (0, 0)))
        across = reduce(lambda running, tap: running + taps_x[tap] * padded[4 - tap: 4 - tap + G], range(5), jnp.zeros_like(beam_image))
        widened = jnp.pad(across, ((0, 0), (2, 2)))
        smooth = reduce(lambda running, tap: running + taps_y[tap] * widened[:, 4 - tap: 4 - tap + G], range(5), jnp.zeros_like(beam_image))
        column_start = (column_shift[beam_number] * column_width).astype(jnp.int32)
        gain_rows = jnp.roll(beam_gain[beam_number], -column_start, axis=0)
        contribution = gain_rows * smooth
        corner = (column_start, row_offset[beam_number].astype(jnp.int32))
        current = lax.dynamic_slice(canvas, corner, (G, G))
        canvas = lax.dynamic_update_slice(canvas, current + contribution, corner)
    return canvas.reshape(2, G, 2 * G)
```

```python
import functools
import math

import jax
import jax.numpy as jnp
import numpy as np
from jax import lax
from jax.experimental import pallas as pl
from jax.experimental.pallas import tpu as pltpu
from jax.sharding import PartitionSpec as P

SIDE = 64
NT = 32
G = 2048
SLOTS = 256
SUBS = 64
SCALE = 3.0
PAD = 8
VMEM_LIMIT = 56 * 1024 * 1024
MESH = pl.DeviceIdType.MESH

f32 = jnp.float32
bf16 = jnp.bfloat16


def split_np(table):
    high = np.asarray(table, np.float32).astype(bf16)
    low = (np.asarray(table, np.float64) - high.astype(np.float64)).astype(np.float32).astype(bf16)
    return high, low


def row_tables():
    x1 = np.arange(NT)[:, None, None]
    x2 = np.arange(SIDE)[None, :, None]
    w = np.arange(SIDE)[None, None, :]
    angle = 2.0 * math.pi * ((w * (NT * x2 + x1)) % G) / G
    high, low = split_np(np.concatenate([np.cos(angle), np.sin(angle)], axis=1))
    return np.concatenate([high, high, low], axis=2)


def column_tables():
    y1 = np.arange(NT)[:, None, None]
    y2 = np.arange(SIDE)[None, :, None]
    r = np.arange(SIDE)[None, None, :]
    angle = 2.0 * math.pi * ((r * (NT * y2 + y1)) % G) / G
    high, low = split_np(np.concatenate([np.cos(angle), -np.sin(angle)], axis=2) / G)
    top = np.concatenate([high, high], axis=2)
    bottom = np.concatenate([low, np.zeros_like(low)], axis=2)
    return np.concatenate([top, bottom], axis=1)


def split(value):
    high = value.astype(bf16)
    low = (value - high.astype(f32)).astype(bf16)
    return high, low


def lane_signs(shape):
    lane = lax.broadcasted_iota(jnp.int32, shape, 1)
    return jnp.where(lane < SIDE, -1.0, 1.0).astype(f32)


def swapped(value):
    return pltpu.roll(value, SIDE, 1)


def transform(parts, signs):
    n = len(parts)
    if n == 1:
        return parts
    even = transform(parts[0::2], signs)
    odd = transform(parts[1::2], signs)
    low, high = [], []
    for k in range(n // 2):
        if k == 0:
            turned = odd[k]
        elif 4 * k == n:
            turned = swapped(odd[k]) * signs
        else:
            angle = 2.0 * math.pi * k / n
            turned = odd[k] * math.cos(angle) + swapped(odd[k]) * (signs * math.sin(angle))
        low.append(even[k] + turned)
        high.append(even[k] - turned)
    return low + high


def transform_leading(source, target):
    signs = lane_signs((8, 2 * SIDE))

    def tile(i, carry):
        at = pl.ds(pl.multiple_of(i * 8, 8), 8)
        for k, value in enumerate(transform([source[q, at, :] for q in range(NT)], signs)):
            target[k, at, :] = value
        return carry

    lax.fori_loop(0, SIDE // 8, tile, 0)


def grid_kernel(
    model, observed, coords, count, block, cell, shift, tap_index, taps, table, out,
    windows, grid, spectrum, padded, rising, falling,
):
    row = lax.broadcasted_iota(jnp.int32, (SIDE, 2 * SIDE), 0).astype(f32)
    rising[...] = jnp.exp(row / SCALE)
    falling[...] = jnp.exp(row / -SCALE)
    left = lax.broadcasted_iota(jnp.int32, (SIDE, 2 * SIDE), 1) < SIDE

    def prepare(pair, carry):
        at = pl.ds(pl.multiple_of(pair * 2 * SIDE, 2 * SIDE), 2 * SIDE)
        for plane in range(2):
            value = model[0, plane, :, at]
            high = value.astype(bf16).astype(f32)
            low = value - high
            rows = pl.ds(plane * SIDE, SIDE)
            windows[2 * pair, rows, :] = jnp.where(left, high, swapped(low)).astype(bf16)
            windows[2 * pair + 1, rows, :] = jnp.where(left, swapped(high), low).astype(bf16)
        return carry

    lax.fori_loop(0, NT // 2, prepare, 0)
    grid[...] = jnp.zeros_like(grid)
    slot = lax.broadcasted_iota(jnp.int32, (2, SLOTS), 1)

    def one(i):
        k = block[0, 0, i]
        q = cell[0, 0, i]
        position = coords[0, k]
        near = jnp.exp(position / -SCALE)
        far = jnp.exp(position / SCALE)
        up = jnp.concatenate([rising[...], rising[...]], axis=1)
        down = jnp.concatenate([falling[...], falling[...]], axis=1)
        along_v = jnp.minimum(up * near[0:1], down * far[0:1])
        along_u = jnp.minimum(up * near[1:2], down * far[1:2])
        high_u, low_u = split(along_u)
        window = windows[q]
        rows = jnp.dot(
            jnp.concatenate([window, window], axis=1),
            jnp.concatenate([high_u, high_u, low_u, low_u], axis=0),
            preferred_element_type=f32,
        )
        predicted = jnp.sum(rows.reshape(2, SIDE, SLOTS) * along_v[None], axis=1)
        residual = jnp.where(slot < count[0, 0, i], observed[0, k] - predicted, 0.0)
        weighted = jnp.concatenate([along_v * residual[0:1], along_v * residual[1:2]], axis=0)
        high_w, low_w = split(weighted)
        products = lax.dot_general(
            jnp.concatenate([high_u, low_u], axis=0),
            jnp.concatenate([high_w, low_w], axis=0),
            (((1,), (1,)), ((), ())),
            preferred_element_type=f32,
        )
        patch = products[:SIDE, : 2 * SIDE] + (
            products[SIDE:, : 2 * SIDE] + products[:SIDE, 2 * SIDE :]
        )
        return q, patch

    def several(i, carry):
        done = [one(i * 4 + j) for j in range(4)]
        for q, patch in done:
            grid[q] += patch
        return carry

    lax.fori_loop(0, SUBS // 4, several, 0)

    transform_leading(grid, spectrum)
    signs = lane_signs((SIDE, 2 * SIDE))
    padded[pl.ds(0, PAD), :] = jnp.zeros((PAD, 2 * SIDE), f32)
    padded[pl.ds(PAD + G, PAD), :] = jnp.zeros((PAD, 2 * SIDE), f32)
    for x1 in range(NT):
        high, low = split(spectrum[x1])
        both = jnp.dot(
            table[x1], jnp.concatenate([high, low, high], axis=0), preferred_element_type=f32
        )
        padded[pl.ds(PAD + x1, SIDE, stride=NT), :] = both[:SIDE] + swapped(both[SIDE:]) * signs

    phase = tap_index[0, 0]
    weights = [taps[phase, tap] for tap in range(5)]
    steps = shift[0]

    def send_block(d, carry):
        start = pl.multiple_of(d * SIDE, SIDE)
        total = weights[0] * padded[pl.ds(start + PAD + 2, SIDE), :]
        for tap in range(1, 5):
            total = total + weights[tap] * padded[pl.ds(start + PAD + 2 - tap, SIDE), :]
        out[(d + steps) % NT] = total
        return carry

    lax.fori_loop(0, NT, send_block, 0)


def image_kernel(columns, gain, offset, tap_index, taps, table, out, spectrum, padded, smooth):
    transform_leading(columns, spectrum)
    zeros = jnp.zeros((PAD, SIDE), f32)
    padded[pl.ds(0, PAD), pl.ds(0, SIDE)] = zeros
    padded[pl.ds(PAD + G, PAD), pl.ds(0, SIDE)] = zeros
    for y1 in range(NT):
        high, low = split(spectrum[y1])
        both = lax.dot_general(
            table[y1],
            jnp.concatenate([high, low], axis=1),
            (((1,), (1,)), ((), ())),
            preferred_element_type=f32,
        )
        padded[pl.ds(PAD + y1, SIDE, stride=NT), pl.ds(0, SIDE)] = both[:SIDE] + both[SIDE:]

    phase = tap_index[0, 1]
    weights = [taps[phase, tap] for tap in range(5)]
    for part in range(G // 128):
        total = weights[0] * padded[pl.ds(part * 128 + PAD + 2, 128), :]
        for tap in range(1, 5):
            total = total + weights[tap] * padded[pl.ds(part * 128 + PAD + 2 - tap, 128), :]
        turned = total.T[:SIDE]
        at = pl.ds(part * 128, 128)
        smooth[:, at] = turned * gain[0, :, at]
    out[...] = pltpu.roll(smooth[...], offset[0], 1)


def exchange_kernel(n, blocks, out, send_sem, recv_sem, own_sem):
    me = lax.axis_index("tile")
    barrier = pltpu.get_barrier_semaphore()
    for step in range(1, n):
        pl.semaphore_signal(
            barrier, inc=1, device_id={"tile": lax.rem(me + step, n)}, device_id_type=MESH
        )
    own = pltpu.make_async_copy(blocks.at[me], out.at[me], own_sem)
    own.start()
    pl.semaphore_wait(barrier, n - 1)
    copies = []
    for step in range(1, n):
        peer = lax.rem(me + step, n)
        copy = pltpu.make_async_remote_copy(
            src_ref=blocks.at[peer],
            dst_ref=out.at[me],
            send_sem=send_sem.at[step],
            recv_sem=recv_sem.at[step],
            device_id={"tile": peer},
            device_id_type=MESH,
        )
        copy.start()
        copies.append(copy)
    own.wait()
    for copy in copies:
        copy.wait()


SMEM = pl.BlockSpec(memory_space=pltpu.SMEM)
VMEM = pl.BlockSpec(memory_space=pltpu.VMEM)
ANY = pl.BlockSpec(memory_space=pl.ANY)


def gridded(model, observed, coords, count, block, cell, shift, tap_index, taps):
    return pl.pallas_call(
        grid_kernel,
        out_shape=jax.ShapeDtypeStruct((NT, SIDE, 2 * SIDE), f32),
        in_specs=[VMEM] * 3 + [SMEM] * 6 + [VMEM],
        out_specs=VMEM,
        scratch_shapes=[
            pltpu.VMEM((NT, 2 * SIDE, 2 * SIDE), bf16),
            pltpu.VMEM((NT, SIDE, 2 * SIDE), f32),
            pltpu.VMEM((NT, SIDE, 2 * SIDE), f32),
            pltpu.VMEM((G + 2 * PAD, 2 * SIDE), f32),
            pltpu.VMEM((SIDE, 2 * SIDE), f32),
            pltpu.VMEM((SIDE, 2 * SIDE), f32),
        ],
        compiler_params=pltpu.CompilerParams(vmem_limit_bytes=VMEM_LIMIT),
        name="grid_rows",
    )(model, observed, coords, count, block, cell, shift, tap_index, taps, jnp.asarray(row_tables()))


def imaged(columns, gain, offset, tap_index, taps):
    return pl.pallas_call(
        image_kernel,
        out_shape=jax.ShapeDtypeStruct((SIDE, G), f32),
        in_specs=[VMEM] * 2 + [SMEM] * 3 + [VMEM],
        out_specs=VMEM,
        scratch_shapes=[
            pltpu.VMEM((NT, SIDE, 2 * SIDE), f32),
            pltpu.VMEM((G + 2 * PAD, 2 * SIDE), f32),
            pltpu.VMEM((SIDE, G), f32),
        ],
        compiler_params=pltpu.CompilerParams(vmem_limit_bytes=VMEM_LIMIT),
        name="image_columns",
    )(columns, gain, offset, tap_index, taps, jnp.asarray(column_tables()))


def exchanged(blocks, n):
    return pl.pallas_call(
        functools.partial(exchange_kernel, n),
        out_shape=jax.ShapeDtypeStruct(blocks.shape, f32),
        in_specs=[VMEM],
        out_specs=VMEM,
        scratch_shapes=[
            pltpu.SemaphoreType.DMA((n,)),
            pltpu.SemaphoreType.DMA((n,)),
            pltpu.SemaphoreType.DMA,
        ],
        compiler_params=pltpu.CompilerParams(
            collective_id=0, has_side_effects=True, vmem_limit_bytes=VMEM_LIMIT
        ),
        name="exchange_tiles",
    )(blocks)


def local(
    model_grid, observed, coords, vis_count, subgrid_block, subgrid_cell, beam_gain,
    column_shift, row_offset, interp_index, interp_taps,
):
    blocks = gridded(
        model_grid, observed, coords, vis_count, subgrid_block, subgrid_cell,
        column_shift, interp_index, interp_taps,
    )
    columns = exchanged(blocks, NT)
    contribution = imaged(columns, beam_gain, row_offset, interp_index, interp_taps)
    tile_index = lax.axis_index("tile")
    upper = tile_index < column_shift[0]
    late = jnp.arange(G, dtype=jnp.int32) < row_offset[0]
    canvas = jnp.concatenate(
        [jnp.where(late, 0.0, contribution), jnp.where(late, contribution, 0.0)], axis=1
    )
    canvas = jnp.stack([jnp.where(upper, 0.0, canvas), jnp.where(upper, canvas, 0.0)])
    return lax.psum_scatter(canvas, "beam", scatter_dimension=2, tiled=True)


def solution(mesh):
    placed = (
        P("beam", None, "tile", None),
        P("beam", "tile", None, None),
        P("beam", "tile", None, None),
        P("beam", "tile", None),
        P("beam", "tile", None),
        P("beam", "tile", None),
        P("beam", "tile", None),
        P("beam"),
        P("beam"),
        P("beam", None),
        P(),
    )
    return jax.shard_map(
        local, mesh=mesh, in_specs=placed, out_specs=P(None, "tile", "beam"), check_vma=False
    )
```

```python
import functools
import math

import jax
import jax.numpy as jnp
import numpy as np
from jax import lax
from jax.experimental import pallas as pl
from jax.experimental.pallas import tpu as pltpu
from jax.sharding import PartitionSpec as P

SIDE = 64
NT = 32
G = 2048
SLOTS = 256
SUBS = 64
SCALE = 3.0
PAD = 8
CHUNK = 512
META = 8
VMEM_LIMIT = 56 * 1024 * 1024
MESH = pl.DeviceIdType.MESH

f32 = jnp.float32
bf16 = jnp.bfloat16


def split_np(table):
    high = np.asarray(table, np.float32).astype(bf16)
    low = (np.asarray(table, np.float64) - high.astype(np.float64)).astype(np.float32).astype(bf16)
    return high, low


def row_tables():
    x1 = np.arange(NT)[:, None, None]
    x2 = np.arange(SIDE)[None, :, None]
    w = np.arange(SIDE)[None, None, :]
    angle = 2.0 * math.pi * ((w * (NT * x2 + x1)) % G) / G
    high, low = split_np(np.concatenate([np.cos(angle), np.sin(angle)], axis=1))
    return np.concatenate([high, high, low], axis=2)


def column_tables():
    y1 = np.arange(NT)[:, None, None]
    y2 = np.arange(SIDE)[None, :, None]
    r = np.arange(SIDE)[None, None, :]
    angle = 2.0 * math.pi * ((r * (NT * y2 + y1)) % G) / G
    high, low = split_np(np.concatenate([np.cos(angle), -np.sin(angle)], axis=2) / G)
    top = np.concatenate([high, high], axis=2)
    bottom = np.concatenate([low, np.zeros_like(low)], axis=2)
    return np.concatenate([top, bottom], axis=1)


def split(value):
    high = value.astype(bf16)
    low = (value - high.astype(f32)).astype(bf16)
    return high, low


def lane_signs(shape):
    lane = lax.broadcasted_iota(jnp.int32, shape, 1)
    return jnp.where(lane < SIDE, -1.0, 1.0).astype(f32)


def swapped(value):
    return pltpu.roll(value, SIDE, 1)


def transform(parts, signs):
    n = len(parts)
    if n == 1:
        return parts
    even = transform(parts[0::2], signs)
    odd = transform(parts[1::2], signs)
    low, high = [], []
    for k in range(n // 2):
        if k == 0:
            turned = odd[k]
        elif 4 * k == n:
            turned = swapped(odd[k]) * signs
        else:
            angle = 2.0 * math.pi * k / n
            turned = odd[k] * math.cos(angle) + swapped(odd[k]) * (signs * math.sin(angle))
        low.append(even[k] + turned)
        high.append(even[k] - turned)
    return low + high


def transform_leading(source, target):
    signs = lane_signs((8, 2 * SIDE))

    def tile(i, carry):
        at = pl.ds(pl.multiple_of(i * 8, 8), 8)
        for k, value in enumerate(transform([source[q, at, :] for q in range(NT)], signs)):
            target[k, at, :] = value
        return carry

    lax.fori_loop(0, SIDE // 8, tile, 0)


def grid_kernel(
    model, observed, coords, count, block, cell, shift, tap_index, taps, table, out,
    windows, grid, spectrum, padded, rising, falling,
):
    row = lax.broadcasted_iota(jnp.int32, (SIDE, 2 * SIDE), 0).astype(f32)
    rising[...] = jnp.exp(row / SCALE)
    falling[...] = jnp.exp(row / -SCALE)
    left = lax.broadcasted_iota(jnp.int32, (SIDE, 2 * SIDE), 1) < SIDE

    def prepare(pair, carry):
        at = pl.ds(pl.multiple_of(pair * 2 * SIDE, 2 * SIDE), 2 * SIDE)
        for plane in range(2):
            value = model[0, plane, :, at]
            high = value.astype(bf16).astype(f32)
            low = value - high
            rows = pl.ds(plane * SIDE, SIDE)
            windows[2 * pair, rows, :] = jnp.where(left, high, swapped(low)).astype(bf16)
            windows[2 * pair + 1, rows, :] = jnp.where(left, swapped(high), low).astype(bf16)
        return carry

    lax.fori_loop(0, NT // 2, prepare, 0)
    grid[...] = jnp.zeros_like(grid)
    slot = lax.broadcasted_iota(jnp.int32, (2, SLOTS), 1)

    def one(i):
        k = block[0, 0, i]
        q = cell[0, 0, i]
        position = coords[0, k]
        near = jnp.exp(position / -SCALE)
        far = jnp.exp(position / SCALE)
        up = jnp.concatenate([rising[...], rising[...]], axis=1)
        down = jnp.concatenate([falling[...], falling[...]], axis=1)
        along_v = jnp.minimum(up * near[0:1], down * far[0:1])
        along_u = jnp.minimum(up * near[1:2], down * far[1:2])
        high_u, low_u = split(along_u)
        window = windows[q]
        rows = jnp.dot(
            jnp.concatenate([window, window], axis=1),
            jnp.concatenate([high_u, high_u, low_u, low_u], axis=0),
            preferred_element_type=f32,
        )
        predicted = jnp.sum(rows.reshape(2, SIDE, SLOTS) * along_v[None], axis=1)
        residual = jnp.where(slot < count[0, 0, i], observed[0, k] - predicted, 0.0)
        weighted = jnp.concatenate([along_v * residual[0:1], along_v * residual[1:2]], axis=0)
        high_w, low_w = split(weighted)
        products = lax.dot_general(
            jnp.concatenate([high_u, low_u], axis=0),
            jnp.concatenate([high_w, low_w], axis=0),
            (((1,), (1,)), ((), ())),
            preferred_element_type=f32,
        )
        patch = products[:SIDE, : 2 * SIDE] + (
            products[SIDE:, : 2 * SIDE] + products[:SIDE, 2 * SIDE :]
        )
        return q, patch

    def several(i, carry):
        done = [one(i * 4 + j) for j in range(4)]
        for q, patch in done:
            grid[q] += patch
        return carry

    lax.fori_loop(0, SUBS // 4, several, 0)

    transform_leading(grid, spectrum)
    signs = lane_signs((SIDE, 2 * SIDE))
    padded[pl.ds(0, PAD), :] = jnp.zeros((PAD, 2 * SIDE), f32)
    padded[pl.ds(PAD + G, PAD), :] = jnp.zeros((PAD, 2 * SIDE), f32)
    for x1 in range(NT):
        high, low = split(spectrum[x1])
        both = jnp.dot(
            table[x1], jnp.concatenate([high, low, high], axis=0), preferred_element_type=f32
        )
        padded[pl.ds(PAD + x1, SIDE, stride=NT), :] = both[:SIDE] + swapped(both[SIDE:]) * signs

    phase = tap_index[0, 0]
    weights = [taps[phase, tap] for tap in range(5)]
    steps = shift[0]

    def send_block(d, carry):
        start = pl.multiple_of(d * SIDE, SIDE)
        total = weights[0] * padded[pl.ds(start + PAD + 2, SIDE), :]
        for tap in range(1, 5):
            total = total + weights[tap] * padded[pl.ds(start + PAD + 2 - tap, SIDE), :]
        out[(d + steps) % NT] = total
        return carry

    lax.fori_loop(0, NT, send_block, 0)


def image_kernel(
    columns, gain, offset, shift, tap_index, taps, table, out, spectrum, padded, smooth
):
    transform_leading(columns, spectrum)
    zeros = jnp.zeros((PAD, SIDE), f32)
    padded[pl.ds(0, PAD), pl.ds(0, SIDE)] = zeros
    padded[pl.ds(PAD + G, PAD), pl.ds(0, SIDE)] = zeros
    for y1 in range(NT):
        high, low = split(spectrum[y1])
        both = lax.dot_general(
            table[y1],
            jnp.concatenate([high, low], axis=1),
            (((1,), (1,)), ((), ())),
            preferred_element_type=f32,
        )
        padded[pl.ds(PAD + y1, SIDE, stride=NT), pl.ds(0, SIDE)] = both[:SIDE] + both[SIDE:]

    phase = tap_index[0, 1]
    weights = [taps[phase, tap] for tap in range(5)]
    for part in range(G // 128):
        total = weights[0] * padded[pl.ds(part * 128 + PAD + 2, 128), :]
        for tap in range(1, 5):
            total = total + weights[tap] * padded[pl.ds(part * 128 + PAD + 2 - tap, 128), :]
        turned = total.T[:SIDE]
        at = pl.ds(part * 128, 128)
        smooth[:, at] = turned * gain[0, :, at]
    rolled = pltpu.roll(smooth[...], offset[0], 1)
    upper = jnp.where(lax.axis_index("tile") < shift[0], 1.0, 0.0)
    first = jnp.full((META, CHUNK), offset[0].astype(f32))
    kind = lax.broadcasted_iota(jnp.int32, (META, CHUNK), 0)
    facts = jnp.where(kind == 0, first, upper)
    for chunk in range(4):
        out[chunk % 2, chunk // 2, pl.ds(0, SIDE), :] = rolled[:, chunk * CHUNK : (chunk + 1) * CHUNK]
        out[chunk % 2, chunk // 2, pl.ds(SIDE, META), :] = facts


def exchange_kernel(n, blocks, out, send_sem, recv_sem, own_sem):
    me = lax.axis_index("tile")
    barrier = pltpu.get_barrier_semaphore()
    for step in range(1, n):
        pl.semaphore_signal(
            barrier, inc=1, device_id={"tile": lax.rem(me + step, n)}, device_id_type=MESH
        )
    own = pltpu.make_async_copy(blocks.at[me], out.at[me], own_sem)
    own.start()
    pl.semaphore_wait(barrier, n - 1)
    copies = []
    for step in range(1, n):
        peer = lax.rem(me + step, n)
        copy = pltpu.make_async_remote_copy(
            src_ref=blocks.at[peer],
            dst_ref=out.at[me],
            send_sem=send_sem.at[step],
            recv_sem=recv_sem.at[step],
            device_id={"tile": peer},
            device_id_type=MESH,
        )
        copy.start()
        copies.append(copy)
    own.wait()
    for copy in copies:
        copy.wait()


def sum_kernel(pieces, out, paired, terms, landed, send_sem, recv_sem):
    beam = lax.axis_index("beam")
    level, core = beam // 2, lax.rem(beam, 2)
    mate = beam + 1 - 2 * core
    up, down = lax.rem(beam + 2, 8), lax.rem(beam + 6, 8)
    barrier = pltpu.get_barrier_semaphore()
    for peer in (mate, up, down):
        pl.semaphore_signal(barrier, inc=1, device_id={"beam": peer}, device_id_type=MESH)
    pl.semaphore_wait(barrier, 3)

    def send(number, source, target, peer):
        copy = pltpu.make_async_remote_copy(
            src_ref=source,
            dst_ref=target,
            send_sem=send_sem.at[number],
            recv_sem=recv_sem.at[number],
            device_id={"beam": peer},
            device_id_type=MESH,
        )
        copy.start()
        return copy

    pair = send(0, pieces.at[1 - core], paired, mate)
    lane = lax.broadcasted_iota(jnp.int32, (1, CHUNK), 1)

    def term(source, half, which):
        part, late = lax.rem(half, 2), half // 2
        row = (lane + CHUNK * (2 * part + core)).astype(f32)
        facts = source[part, pl.ds(SIDE, META), :]
        is_late = jnp.where(row < facts[0:1], 1, 0)
        here = (is_late == late) & (facts[1:2] == float(which))
        return jnp.where(here, source[part, pl.ds(0, SIDE), :], 0.0)

    own = pieces.at[core]
    pair.wait_recv()

    def both(half, which):
        return term(own, half, which) + term(paired, half, which)

    far, above, below = lax.rem(level + 2, 4), lax.rem(level + 1, 4), lax.rem(level + 3, 4)
    terms[0] = both(far, 0)
    far_up = send(1, terms.at[0], landed.at[0], up)
    terms[1] = both(far, 1)
    far_down = send(2, terms.at[1], landed.at[1], down)
    terms[2] = both(above, 1)
    near_up = send(3, terms.at[2], landed.at[2], up)
    terms[3] = both(below, 0)
    near_down = send(4, terms.at[3], landed.at[3], down)
    terms[4] = both(above, 0)
    terms[5] = both(below, 1)
    far_up.wait_recv()
    terms[4] += landed[0]
    last_up = send(5, terms.at[4], landed.at[4], up)
    far_down.wait_recv()
    terms[5] += landed[1]
    last_down = send(6, terms.at[5], landed.at[5], down)
    out[0] = both(level, 0)
    out[1] = both(level, 1)
    near_up.wait_recv()
    out[1] += landed[2]
    near_down.wait_recv()
    out[0] += landed[3]
    last_up.wait_recv()
    out[0] += landed[4]
    last_down.wait_recv()
    out[1] += landed[5]
    for copy in (pair, far_up, far_down, near_up, near_down, last_up, last_down):
        copy.wait_send()


SMEM = pl.BlockSpec(memory_space=pltpu.SMEM)
VMEM = pl.BlockSpec(memory_space=pltpu.VMEM)
ANY = pl.BlockSpec(memory_space=pl.ANY)


def gridded(model, observed, coords, count, block, cell, shift, tap_index, taps):
    return pl.pallas_call(
        grid_kernel,
        out_shape=jax.ShapeDtypeStruct((NT, SIDE, 2 * SIDE), f32),
        in_specs=[VMEM] * 3 + [SMEM] * 6 + [VMEM],
        out_specs=VMEM,
        scratch_shapes=[
            pltpu.VMEM((NT, 2 * SIDE, 2 * SIDE), bf16),
            pltpu.VMEM((NT, SIDE, 2 * SIDE), f32),
            pltpu.VMEM((NT, SIDE, 2 * SIDE), f32),
            pltpu.VMEM((G + 2 * PAD, 2 * SIDE), f32),
            pltpu.VMEM((SIDE, 2 * SIDE), f32),
            pltpu.VMEM((SIDE, 2 * SIDE), f32),
        ],
        compiler_params=pltpu.CompilerParams(vmem_limit_bytes=VMEM_LIMIT),
        name="grid_rows",
    )(model, observed, coords, count, block, cell, shift, tap_index, taps, jnp.asarray(row_tables()))


def imaged(columns, gain, offset, shift, tap_index, taps):
    return pl.pallas_call(
        image_kernel,
        out_shape=jax.ShapeDtypeStruct((2, 2, SIDE + META, CHUNK), f32),
        in_specs=[VMEM] * 2 + [SMEM] * 4 + [VMEM],
        out_specs=VMEM,
        scratch_shapes=[
            pltpu.VMEM((NT, SIDE, 2 * SIDE), f32),
            pltpu.VMEM((G + 2 * PAD, 2 * SIDE), f32),
            pltpu.VMEM((SIDE, G), f32),
        ],
        compiler_params=pltpu.CompilerParams(vmem_limit_bytes=VMEM_LIMIT),
        name="image_columns",
    )(columns, gain, offset, shift, tap_index, taps, jnp.asarray(column_tables()))


def exchanged(blocks, n):
    return pl.pallas_call(
        functools.partial(exchange_kernel, n),
        out_shape=jax.ShapeDtypeStruct(blocks.shape, f32),
        in_specs=[VMEM],
        out_specs=VMEM,
        scratch_shapes=[
            pltpu.SemaphoreType.DMA((n,)),
            pltpu.SemaphoreType.DMA((n,)),
            pltpu.SemaphoreType.DMA,
        ],
        compiler_params=pltpu.CompilerParams(
            collective_id=0, has_side_effects=True, vmem_limit_bytes=VMEM_LIMIT
        ),
        name="exchange_tiles",
    )(blocks)


def summed(pieces):
    return pl.pallas_call(
        sum_kernel,
        out_shape=jax.ShapeDtypeStruct((2, SIDE, CHUNK), f32),
        in_specs=[VMEM],
        out_specs=VMEM,
        scratch_shapes=[
            pltpu.VMEM((2, SIDE + META, CHUNK), f32),
            pltpu.VMEM((6, SIDE, CHUNK), f32),
            pltpu.VMEM((6, SIDE, CHUNK), f32),
            pltpu.SemaphoreType.DMA((7,)),
            pltpu.SemaphoreType.DMA((7,)),
        ],
        compiler_params=pltpu.CompilerParams(
            collective_id=1, has_side_effects=True, vmem_limit_bytes=VMEM_LIMIT
        ),
        name="sum_beams",
    )(pieces)


def local(
    model_grid, observed, coords, vis_count, subgrid_block, subgrid_cell, beam_gain,
    column_shift, row_offset, interp_index, interp_taps,
):
    blocks = gridded(
        model_grid, observed, coords, vis_count, subgrid_block, subgrid_cell,
        column_shift, interp_index, interp_taps,
    )
    columns = exchanged(blocks, NT)
    pieces = imaged(columns, beam_gain, row_offset, column_shift, interp_index, interp_taps)
    return summed(pieces)


def solution(mesh):
    placed = (
        P("beam", None, "tile", None),
        P("beam", "tile", None, None),
        P("beam", "tile", None, None),
        P("beam", "tile", None),
        P("beam", "tile", None),
        P("beam", "tile", None),
        P("beam", "tile", None),
        P("beam"),
        P("beam"),
        P("beam", None),
        P(),
    )
    return jax.shard_map(
        local, mesh=mesh, in_specs=placed, out_specs=P(None, "tile", "beam"), check_vma=False
    )
```

```python
import math

import jax
import jax.numpy as jnp
import numpy as np
from jax import lax
from jax.experimental import pallas as pl
from jax.experimental.pallas import tpu as pltpu
from jax.sharding import PartitionSpec as P

SIDE = 64
NT = 32
G = 2048
SLOTS = 256
SUBS = 64
SCALE = 3.0
PAD = 8
BEAMS = 8
CHUNK = 512
GROUPS = 4
ROWS = SIDE // GROUPS
META = 8
VMEM_LIMIT = 56 * 1024 * 1024
MESH = pl.DeviceIdType.MESH

f32 = jnp.float32
bf16 = jnp.bfloat16


def split_np(table):
    high = np.asarray(table, np.float32).astype(bf16)
    low = (np.asarray(table, np.float64) - high.astype(np.float64)).astype(np.float32).astype(bf16)
    return high, low


def row_tables():
    x1 = np.arange(NT)[:, None, None]
    x2 = np.arange(SIDE)[None, :, None]
    w = np.arange(SIDE)[None, None, :]
    angle = 2.0 * math.pi * ((w * (NT * x2 + x1)) % G) / G
    high, low = split_np(np.concatenate([np.cos(angle), np.sin(angle)], axis=1))
    return np.concatenate([high, high, low], axis=2)


def column_tables():
    y1 = np.arange(NT)[:, None, None]
    y2 = np.arange(SIDE)[None, :, None]
    r = np.arange(SIDE)[None, None, :]
    angle = 2.0 * math.pi * ((r * (NT * y2 + y1)) % G) / G
    high, low = split_np(np.concatenate([np.cos(angle), -np.sin(angle)], axis=2) / G)
    top = np.concatenate([high, high], axis=2)
    bottom = np.concatenate([low, np.zeros_like(low)], axis=2)
    return np.concatenate([top, bottom], axis=1)


def split(value):
    high = value.astype(bf16)
    low = (value - high.astype(f32)).astype(bf16)
    return high, low


def lane_signs(shape):
    lane = lax.broadcasted_iota(jnp.int32, shape, 1)
    return jnp.where(lane < SIDE, -1.0, 1.0).astype(f32)


def swapped(value):
    return pltpu.roll(value, SIDE, 1)


def transform(parts, signs):
    n = len(parts)
    if n == 1:
        return parts
    even = transform(parts[0::2], signs)
    odd = transform(parts[1::2], signs)
    low, high = [], []
    for k in range(n // 2):
        if k == 0:
            turned = odd[k]
        elif 4 * k == n:
            turned = swapped(odd[k]) * signs
        else:
            angle = 2.0 * math.pi * k / n
            turned = odd[k] * math.cos(angle) + swapped(odd[k]) * (signs * math.sin(angle))
        low.append(even[k] + turned)
        high.append(even[k] - turned)
    return low + high


def transform_leading(source, target):
    signs = lane_signs((8, 2 * SIDE))

    def tile(i, carry):
        at = pl.ds(pl.multiple_of(i * 8, 8), 8)
        for k, value in enumerate(transform([source[q, at, :] for q in range(NT)], signs)):
            target[k, at, :] = value
        return carry

    lax.fori_loop(0, SIDE // 8, tile, 0)


def grid_kernel(
    model, observed, coords, count, block, cell, shift, tap_index, taps, table, out,
    windows, grid, spectrum, padded, rising, falling,
):
    row = lax.broadcasted_iota(jnp.int32, (SIDE, 2 * SIDE), 0).astype(f32)
    rising[...] = jnp.exp(row / SCALE)
    falling[...] = jnp.exp(row / -SCALE)
    left = lax.broadcasted_iota(jnp.int32, (SIDE, 2 * SIDE), 1) < SIDE

    def prepare(pair, carry):
        at = pl.ds(pl.multiple_of(pair * 2 * SIDE, 2 * SIDE), 2 * SIDE)
        for plane in range(2):
            value = model[0, plane, :, at]
            high = value.astype(bf16).astype(f32)
            low = value - high
            rows = pl.ds(plane * SIDE, SIDE)
            windows[2 * pair, rows, :] = jnp.where(left, high, swapped(low)).astype(bf16)
            windows[2 * pair + 1, rows, :] = jnp.where(left, swapped(high), low).astype(bf16)
        return carry

    lax.fori_loop(0, NT // 2, prepare, 0)
    grid[...] = jnp.zeros_like(grid)
    slot = lax.broadcasted_iota(jnp.int32, (2, SLOTS), 1)

    def one(i):
        k = block[0, 0, i]
        q = cell[0, 0, i]
        position = coords[0, k]
        near = jnp.exp(position / -SCALE)
        far = jnp.exp(position / SCALE)
        up = jnp.concatenate([rising[...], rising[...]], axis=1)
        down = jnp.concatenate([falling[...], falling[...]], axis=1)
        along_v = jnp.minimum(up * near[0:1], down * far[0:1])
        along_u = jnp.minimum(up * near[1:2], down * far[1:2])
        high_u, low_u = split(along_u)
        window = windows[q]
        rows = jnp.dot(
            jnp.concatenate([window, window], axis=1),
            jnp.concatenate([high_u, high_u, low_u, low_u], axis=0),
            preferred_element_type=f32,
        )
        predicted = jnp.sum(rows.reshape(2, SIDE, SLOTS) * along_v[None], axis=1)
        residual = jnp.where(slot < count[0, 0, i], observed[0, k] - predicted, 0.0)
        weighted = jnp.concatenate([along_v * residual[0:1], along_v * residual[1:2]], axis=0)
        high_w, low_w = split(weighted)
        products = lax.dot_general(
            jnp.concatenate([high_u, low_u], axis=0),
            jnp.concatenate([high_w, low_w], axis=0),
            (((1,), (1,)), ((), ())),
            preferred_element_type=f32,
        )
        patch = products[:SIDE, : 2 * SIDE] + (
            products[SIDE:, : 2 * SIDE] + products[:SIDE, 2 * SIDE :]
        )
        return q, patch

    def several(i, carry):
        done = [one(i * 4 + j) for j in range(4)]
        for q, patch in done:
            grid[q] += patch
        return carry

    lax.fori_loop(0, SUBS // 4, several, 0)

    transform_leading(grid, spectrum)
    signs = lane_signs((SIDE, 2 * SIDE))
    padded[pl.ds(0, PAD), :] = jnp.zeros((PAD, 2 * SIDE), f32)
    padded[pl.ds(PAD + G, PAD), :] = jnp.zeros((PAD, 2 * SIDE), f32)
    for x1 in range(NT):
        high, low = split(spectrum[x1])
        both = jnp.dot(
            table[x1], jnp.concatenate([high, low, high], axis=0), preferred_element_type=f32
        )
        padded[pl.ds(PAD + x1, SIDE, stride=NT), :] = both[:SIDE] + swapped(both[SIDE:]) * signs

    phase = tap_index[0, 0]
    weights = [taps[phase, tap] for tap in range(5)]
    steps = shift[0]

    def send_block(d, carry):
        start = pl.multiple_of(d * SIDE, SIDE)
        total = weights[0] * padded[pl.ds(start + PAD + 2, SIDE), :]
        for tap in range(1, 5):
            total = total + weights[tap] * padded[pl.ds(start + PAD + 2 - tap, SIDE), :]
        out[(d + steps) % NT] = total
        return carry

    lax.fori_loop(0, NT, send_block, 0)


def tail_kernel(
    blocks, gain, offset, shift, tap_index, taps, table, out,
    landing, spectrum, padded, smooth, pieces, paired, terms, landed,
    own_sem, tile_send, tile_recv, pair_send, pair_recv, ring_send, ring_recv,
):
    me = lax.axis_index("tile")
    beam = lax.axis_index("beam")
    level, core = beam // 2, lax.rem(beam, 2)
    mate = beam + 1 - 2 * core
    up, down = lax.rem(beam + 2, BEAMS), lax.rem(beam + 6, BEAMS)
    barrier = pltpu.get_barrier_semaphore()
    for step in range(1, NT):
        pl.semaphore_signal(
            barrier, inc=1, device_id={"tile": lax.rem(me + step, NT)}, device_id_type=MESH
        )
    for peer in (mate, up, down):
        pl.semaphore_signal(barrier, inc=1, device_id={"beam": peer}, device_id_type=MESH)
    own = pltpu.make_async_copy(blocks.at[me], landing.at[me], own_sem)
    own.start()
    padded[pl.ds(0, PAD), :] = jnp.zeros((PAD, 2 * SIDE), f32)
    padded[pl.ds(PAD + G, PAD), :] = jnp.zeros((PAD, 2 * SIDE), f32)
    pl.semaphore_wait(barrier, NT + 2)

    def rows_of(g):
        return pl.ds(pl.multiple_of(g * ROWS, ROWS), ROWS)

    def send_group(g, carry):
        def send_one(step, inner):
            peer = lax.rem(me + step, NT)
            pltpu.make_async_remote_copy(
                src_ref=blocks.at[peer, rows_of(g)],
                dst_ref=landing.at[me, rows_of(g)],
                send_sem=tile_send.at[g],
                recv_sem=tile_recv.at[g],
                device_id={"tile": peer},
                device_id_type=MESH,
            ).start()
            return inner

        return lax.fori_loop(1, NT, send_one, carry)

    lax.fori_loop(0, GROUPS, send_group, 0)
    own.wait()

    def wait_group(g, semaphores):
        most = pl.ds(0, NT - 1)
        pltpu.make_async_copy(
            blocks.at[most, rows_of(g)], landing.at[most, rows_of(g)], semaphores.at[g]
        ).wait()

    phase = tap_index[0, 1]
    weights = [taps[phase, tap] for tap in range(5)]
    signs = lane_signs((8, 2 * SIDE))
    upper = jnp.where(me < shift[0], 1.0, 0.0)
    first = jnp.full((META, CHUNK), offset[0].astype(f32))
    kind = lax.broadcasted_iota(jnp.int32, (META, CHUNK), 0)
    facts = jnp.where(kind == 0, first, upper)

    def image_group(g):
        def tile(i, carry):
            start = pl.multiple_of(g * ROWS + i * 8, 8)
            values = transform([landing[t, pl.ds(start, 8), :] for t in range(NT)], signs)
            at = pl.ds(pl.multiple_of(i * 8, 8), 8)
            for y1, value in enumerate(values):
                spectrum[y1, at, :] = value
            return carry

        lax.fori_loop(0, ROWS // 8, tile, 0)
        for y1 in range(NT):
            high, low = split(spectrum[y1])
            both = lax.dot_general(
                table[y1],
                jnp.concatenate([high, low], axis=1),
                (((1,), (1,)), ((), ())),
                preferred_element_type=f32,
            )
            padded[pl.ds(PAD + y1, SIDE, stride=NT), pl.ds(0, ROWS)] = both[:SIDE] + both[SIDE:]
        for part in range(G // 128):
            total = weights[0] * padded[pl.ds(part * 128 + PAD + 2, 128), :]
            for tap in range(1, 5):
                total = total + weights[tap] * padded[pl.ds(part * 128 + PAD + 2 - tap, 128), :]
            at = pl.ds(part * 128, 128)
            smooth[:, at] = total.T[:ROWS] * gain[0, rows_of(g), at]
        rolled = pltpu.roll(smooth[...], offset[0], 1)
        for chunk in range(4):
            piece = rolled[:, chunk * CHUNK : (chunk + 1) * CHUNK]
            pieces[g, chunk % 2, chunk // 2, pl.ds(0, ROWS), :] = piece
            pieces[g, chunk % 2, chunk // 2, pl.ds(ROWS, META), :] = facts

    def pair(g):
        return pltpu.make_async_remote_copy(
            src_ref=pieces.at[g, 1 - core],
            dst_ref=paired.at[g],
            send_sem=pair_send.at[g],
            recv_sem=pair_recv.at[g],
            device_id={"beam": mate},
            device_id_type=MESH,
        )

    def ring(g, number, peer):
        return pltpu.make_async_remote_copy(
            src_ref=terms.at[g, number],
            dst_ref=landed.at[g, number],
            send_sem=ring_send.at[g, number],
            recv_sem=ring_recv.at[g, number],
            device_id={"beam": peer},
            device_id_type=MESH,
        )

    lane = lax.broadcasted_iota(jnp.int32, (1, CHUNK), 1)

    def term(source, half, which):
        part, late = lax.rem(half, 2), half // 2
        row = (lane + CHUNK * (2 * part + core)).astype(f32)
        told = source[part, pl.ds(ROWS, META), :]
        is_late = jnp.where(row < told[0:1], 1, 0)
        here = (is_late == late) & (told[1:2] == float(which))
        return jnp.where(here, source[part, pl.ds(0, ROWS), :], 0.0)

    def both_terms(g, half, which):
        return term(pieces.at[g, core], half, which) + term(paired.at[g], half, which)

    far, above, below = lax.rem(level + 2, 4), lax.rem(level + 1, 4), lax.rem(level + 3, 4)
    peers = (up, down, up, down, up, down)

    def first_hop(g):
        pair(g).wait_recv()
        for number, half, which in ((0, far, 0), (1, far, 1), (2, above, 1), (3, below, 0)):
            terms[g, number] = both_terms(g, half, which)
            ring(g, number, peers[number]).start()
        terms[g, 4] = both_terms(g, above, 0)
        terms[g, 5] = both_terms(g, below, 1)

    def second_hop(g):
        for number in (0, 1):
            ring(g, number, peers[number]).wait_recv()
            terms[g, 4 + number] += landed[g, number]
            ring(g, 4 + number, peers[4 + number]).start()

    def group(g, carry):
        wait_group(g, tile_recv)
        image_group(g)
        pair(g).start()

        @pl.when(g > 0)
        def _():
            second_hop(g - 1)

        first_hop(g)
        return carry

    lax.fori_loop(0, GROUPS, group, 0)
    second_hop(GROUPS - 1)

    def finish(g, carry):
        wait_group(g, tile_send)
        pair(g).wait_send()
        for which in (0, 1):
            total = both_terms(g, level, which)
            for number in (3 - which, 4 + which):
                ring(g, number, peers[number]).wait_recv()
                total += landed[g, number]
            out[which, rows_of(g), :] = total
        for number in range(6):
            ring(g, number, peers[number]).wait_send()
        return carry

    lax.fori_loop(0, GROUPS, finish, 0)


SMEM = pl.BlockSpec(memory_space=pltpu.SMEM)
VMEM = pl.BlockSpec(memory_space=pltpu.VMEM)
ANY = pl.BlockSpec(memory_space=pl.ANY)


def gridded(model, observed, coords, count, block, cell, shift, tap_index, taps):
    return pl.pallas_call(
        grid_kernel,
        out_shape=jax.ShapeDtypeStruct((NT, SIDE, 2 * SIDE), f32),
        in_specs=[VMEM] * 3 + [SMEM] * 6 + [VMEM],
        out_specs=VMEM,
        scratch_shapes=[
            pltpu.VMEM((NT, 2 * SIDE, 2 * SIDE), bf16),
            pltpu.VMEM((NT, SIDE, 2 * SIDE), f32),
            pltpu.VMEM((NT, SIDE, 2 * SIDE), f32),
            pltpu.VMEM((G + 2 * PAD, 2 * SIDE), f32),
            pltpu.VMEM((SIDE, 2 * SIDE), f32),
            pltpu.VMEM((SIDE, 2 * SIDE), f32),
        ],
        compiler_params=pltpu.CompilerParams(vmem_limit_bytes=VMEM_LIMIT),
        name="grid_rows",
    )(model, observed, coords, count, block, cell, shift, tap_index, taps, jnp.asarray(row_tables()))


def finished(blocks, gain, offset, shift, tap_index, taps):
    return pl.pallas_call(
        tail_kernel,
        out_shape=jax.ShapeDtypeStruct((2, SIDE, CHUNK), f32),
        in_specs=[VMEM] * 2 + [SMEM] * 4 + [VMEM],
        out_specs=VMEM,
        scratch_shapes=[
            pltpu.VMEM((NT, SIDE, 2 * SIDE), f32),
            pltpu.VMEM((NT, ROWS, 2 * SIDE), f32),
            pltpu.VMEM((G + 2 * PAD, 2 * SIDE), f32),
            pltpu.VMEM((ROWS, G), f32),
            pltpu.VMEM((GROUPS, 2, 2, ROWS + META, CHUNK), f32),
            pltpu.VMEM((GROUPS, 2, ROWS + META, CHUNK), f32),
            pltpu.VMEM((GROUPS, 6, ROWS, CHUNK), f32),
            pltpu.VMEM((GROUPS, 6, ROWS, CHUNK), f32),
            pltpu.SemaphoreType.DMA,
            pltpu.SemaphoreType.DMA((GROUPS,)),
            pltpu.SemaphoreType.DMA((GROUPS,)),
            pltpu.SemaphoreType.DMA((GROUPS,)),
            pltpu.SemaphoreType.DMA((GROUPS,)),
            pltpu.SemaphoreType.DMA((GROUPS, 6)),
            pltpu.SemaphoreType.DMA((GROUPS, 6)),
        ],
        compiler_params=pltpu.CompilerParams(
            collective_id=0, has_side_effects=True, vmem_limit_bytes=VMEM_LIMIT
        ),
        name="image_and_sum",
    )(blocks, gain, offset, shift, tap_index, taps, jnp.asarray(column_tables()))


def local(
    model_grid, observed, coords, vis_count, subgrid_block, subgrid_cell, beam_gain,
    column_shift, row_offset, interp_index, interp_taps,
):
    blocks = gridded(
        model_grid, observed, coords, vis_count, subgrid_block, subgrid_cell,
        column_shift, interp_index, interp_taps,
    )
    return finished(blocks, beam_gain, row_offset, column_shift, interp_index, interp_taps)


def solution(mesh):
    placed = (
        P("beam", None, "tile", None),
        P("beam", "tile", None, None),
        P("beam", "tile", None, None),
        P("beam", "tile", None),
        P("beam", "tile", None),
        P("beam", "tile", None),
        P("beam", "tile", None),
        P("beam"),
        P("beam"),
        P("beam", None),
        P(),
    )
    return jax.shard_map(
        local, mesh=mesh, in_specs=placed, out_specs=P(None, "tile", "beam"), check_vma=False
    )
```

```python
import math

import jax
import jax.numpy as jnp
import numpy as np
from jax import lax
from jax.experimental import pallas as pl
from jax.experimental.pallas import tpu as pltpu
from jax.sharding import PartitionSpec as P

SIDE = 64
NT = 32
G = 2048
SLOTS = 256
SUBS = 64
SCALE = 3.0
PAD = 8
BEAMS = 8
CHUNK = 512
GROUPS = 4
ROWS = SIDE // GROUPS
META = 8
VMEM_LIMIT = 56 * 1024 * 1024
MESH = pl.DeviceIdType.MESH

f32 = jnp.float32
bf16 = jnp.bfloat16


def split_np(table):
    high = np.asarray(table, np.float32).astype(bf16)
    low = (np.asarray(table, np.float64) - high.astype(np.float64)).astype(np.float32).astype(bf16)
    return high, low


def row_tables():
    x1 = np.arange(NT)[:, None, None]
    x2 = np.arange(SIDE)[None, :, None]
    w = np.arange(SIDE)[None, None, :]
    angle = 2.0 * math.pi * ((w * (NT * x2 + x1)) % G) / G
    high, low = split_np(np.concatenate([np.cos(angle), np.sin(angle)], axis=1))
    return np.concatenate([high, high, low], axis=2)


def column_tables():
    y1 = np.arange(NT)[:, None, None]
    y2 = np.arange(SIDE)[None, :, None]
    r = np.arange(SIDE)[None, None, :]
    angle = 2.0 * math.pi * ((r * (NT * y2 + y1)) % G) / G
    high, low = split_np(np.concatenate([np.cos(angle), -np.sin(angle)], axis=2) / G)
    top = np.concatenate([high, high], axis=2)
    bottom = np.concatenate([low, np.zeros_like(low)], axis=2)
    return np.concatenate([top, bottom], axis=1)


def split(value):
    high = value.astype(bf16)
    low = (value - high.astype(f32)).astype(bf16)
    return high, low


def lane_signs(shape):
    lane = lax.broadcasted_iota(jnp.int32, shape, 1)
    return jnp.where(lane < SIDE, -1.0, 1.0).astype(f32)


def swapped(value):
    return pltpu.roll(value, SIDE, 1)


def transform(parts, signs):
    n = len(parts)
    if n == 1:
        return parts
    even = transform(parts[0::2], signs)
    odd = transform(parts[1::2], signs)
    low, high = [], []
    for k in range(n // 2):
        if k == 0:
            turned = odd[k]
        elif 4 * k == n:
            turned = swapped(odd[k]) * signs
        else:
            angle = 2.0 * math.pi * k / n
            turned = odd[k] * math.cos(angle) + swapped(odd[k]) * (signs * math.sin(angle))
        low.append(even[k] + turned)
        high.append(even[k] - turned)
    return low + high


def grid_kernel(
    model, observed, coords, count, block, cell, grid, windows, rising, falling
):
    row = lax.broadcasted_iota(jnp.int32, (SIDE, 2 * SIDE), 0).astype(f32)
    rising[...] = jnp.exp(row / SCALE)
    falling[...] = jnp.exp(row / -SCALE)
    left = lax.broadcasted_iota(jnp.int32, (SIDE, 2 * SIDE), 1) < SIDE

    def prepare(pair, carry):
        at = pl.ds(pl.multiple_of(pair * 2 * SIDE, 2 * SIDE), 2 * SIDE)
        for plane in range(2):
            value = model[0, plane, :, at]
            high = value.astype(bf16).astype(f32)
            low = value - high
            rows = pl.ds(plane * SIDE, SIDE)
            windows[2 * pair, rows, :] = jnp.where(left, high, swapped(low)).astype(bf16)
            windows[2 * pair + 1, rows, :] = jnp.where(left, swapped(high), low).astype(bf16)
        return carry

    lax.fori_loop(0, NT // 2, prepare, 0)
    grid[...] = jnp.zeros_like(grid)
    slot = lax.broadcasted_iota(jnp.int32, (2, SLOTS), 1)

    def one(i):
        k = block[0, 0, i]
        q = cell[0, 0, i]
        position = coords[0, k]
        near = jnp.exp(position / -SCALE)
        far = jnp.exp(position / SCALE)
        up = jnp.concatenate([rising[...], rising[...]], axis=1)
        down = jnp.concatenate([falling[...], falling[...]], axis=1)
        along_v = jnp.minimum(up * near[0:1], down * far[0:1])
        along_u = jnp.minimum(up * near[1:2], down * far[1:2])
        high_u, low_u = split(along_u)
        window = windows[q]
        rows = jnp.dot(
            jnp.concatenate([window, window], axis=1),
            jnp.concatenate([high_u, high_u, low_u, low_u], axis=0),
            preferred_element_type=f32,
        )
        predicted = jnp.sum(rows.reshape(2, SIDE, SLOTS) * along_v[None], axis=1)
        residual = jnp.where(slot < count[0, 0, i], observed[0, k] - predicted, 0.0)
        weighted = jnp.concatenate([along_v * residual[0:1], along_v * residual[1:2]], axis=0)
        high_w, low_w = split(weighted)
        products = lax.dot_general(
            jnp.concatenate([high_u, low_u], axis=0),
            jnp.concatenate([high_w, low_w], axis=0),
            (((1,), (1,)), ((), ())),
            preferred_element_type=f32,
        )
        patch = products[:SIDE, : 2 * SIDE] + (
            products[SIDE:, : 2 * SIDE] + products[:SIDE, 2 * SIDE :]
        )
        return q, patch

    def several(i, carry):
        done = [one(i * 4 + j) for j in range(4)]
        for q, patch in done:
            grid[q] += patch
        return carry

    lax.fori_loop(0, SUBS // 4, several, 0)


def tail_kernel(
    grid, gain_in, offset, shift, tap_index, taps, row_table_in, table_in, out,
    row_table, table, gain, tapped, blocks, landing, spectrum, padded, smooth,
    pieces, paired, terms, landed,
    in_sem, tile_send, tile_recv, pair_send, pair_recv, ring_send, ring_recv,
):
    me = lax.axis_index("tile")
    beam = lax.axis_index("beam")
    level, core = beam // 2, lax.rem(beam, 2)
    mate = beam + 1 - 2 * core
    up, down = lax.rem(beam + 2, BEAMS), lax.rem(beam + 6, BEAMS)
    barrier = pltpu.get_barrier_semaphore()
    for step in range(1, NT):
        pl.semaphore_signal(
            barrier, inc=1, device_id={"tile": lax.rem(me + step, NT)}, device_id_type=MESH
        )
    for peer in (mate, up, down):
        pl.semaphore_signal(barrier, inc=1, device_id={"beam": peer}, device_id_type=MESH)
    row_copy = pltpu.make_async_copy(row_table_in, row_table, in_sem.at[0])
    row_copy.start()
    column_copy = pltpu.make_async_copy(table_in, table, in_sem.at[1])
    column_copy.start()
    gain_copy = pltpu.make_async_copy(gain_in, gain, in_sem.at[2])
    gain_copy.start()

    signs = lane_signs((8, 2 * SIDE))

    def transform_rows(source, start, rows):
        def tile(i, carry):
            at = pl.ds(pl.multiple_of(start + i * 8, 8), 8)
            to = pl.ds(pl.multiple_of(i * 8, 8), 8)
            for k, value in enumerate(transform([source[t, at, :] for t in range(NT)], signs)):
                spectrum[k, to, :] = value
            return carry

        lax.fori_loop(0, rows // 8, tile, 0)

    padded[pl.ds(0, PAD), :] = jnp.zeros((PAD, 2 * SIDE), f32)
    padded[pl.ds(PAD + G, PAD), :] = jnp.zeros((PAD, 2 * SIDE), f32)
    transform_rows(grid, 0, SIDE)
    row_copy.wait()
    wide_signs = lane_signs((SIDE, 2 * SIDE))
    for x1 in range(NT):
        high, low = split(spectrum[x1])
        both = jnp.dot(
            row_table[x1], jnp.concatenate([high, low, high], axis=0), preferred_element_type=f32
        )
        padded[pl.ds(PAD + x1, SIDE, stride=NT), :] = both[:SIDE] + swapped(both[SIDE:]) * wide_signs

    def rows_of(g):
        return pl.ds(pl.multiple_of(g * ROWS, ROWS), ROWS)

    phase_x = tap_index[0, 0]
    weights_x = [taps[phase_x, tap] for tap in range(5)]
    steps = shift[0]

    def make_group(g):
        def make(d, carry):
            start = pl.multiple_of(d * SIDE + g * ROWS, ROWS)
            total = weights_x[0] * padded[pl.ds(start + PAD + 2, ROWS), :]
            for tap in range(1, 5):
                total = total + weights_x[tap] * padded[pl.ds(start + PAD + 2 - tap, ROWS), :]
            tapped[d] = total
            return carry

        def place(d, carry):
            blocks[d, rows_of(g), :] = tapped[lax.rem(d - steps + NT, NT)]
            return carry

        lax.fori_loop(0, NT, make, 0)
        lax.fori_loop(0, NT, place, 0)
        landing[me, rows_of(g), :] = blocks[me, rows_of(g), :]

    def send_group(g):
        def send_one(step, inner):
            peer = lax.rem(me + step, NT)
            pltpu.make_async_remote_copy(
                src_ref=blocks.at[peer, rows_of(g)],
                dst_ref=landing.at[me, rows_of(g)],
                send_sem=tile_send.at[g],
                recv_sem=tile_recv.at[g],
                device_id={"tile": peer},
                device_id_type=MESH,
            ).start()
            return inner

        lax.fori_loop(1, NT, send_one, 0)

    make_group(0)
    pl.semaphore_wait(barrier, NT + 2)

    def start_group(g, carry):
        send_group(g)

        @pl.when(g < GROUPS - 1)
        def _():
            make_group(g + 1)

        return carry

    lax.fori_loop(0, GROUPS, start_group, 0)
    column_copy.wait()
    gain_copy.wait()

    def wait_group(g, semaphores):
        most = pl.ds(0, NT - 1)
        pltpu.make_async_copy(
            blocks.at[most, rows_of(g)], landing.at[most, rows_of(g)], semaphores.at[g]
        ).wait()

    phase = tap_index[0, 1]
    weights = [taps[phase, tap] for tap in range(5)]
    upper = jnp.where(me < shift[0], 1.0, 0.0)
    first = jnp.full((META, CHUNK), offset[0].astype(f32))
    kind = lax.broadcasted_iota(jnp.int32, (META, CHUNK), 0)
    facts = jnp.where(kind == 0, first, upper)

    def image_group(g):
        transform_rows(landing, g * ROWS, ROWS)
        for y1 in range(NT):
            high, low = split(spectrum[y1, pl.ds(0, ROWS), :])
            both = lax.dot_general(
                table[y1],
                jnp.concatenate([high, low], axis=1),
                (((1,), (1,)), ((), ())),
                preferred_element_type=f32,
            )
            padded[pl.ds(PAD + y1, SIDE, stride=NT), pl.ds(0, ROWS)] = both[:SIDE] + both[SIDE:]
        for part in range(G // 128):
            total = weights[0] * padded[pl.ds(part * 128 + PAD + 2, 128), :]
            for tap in range(1, 5):
                total = total + weights[tap] * padded[pl.ds(part * 128 + PAD + 2 - tap, 128), :]
            at = pl.ds(part * 128, 128)
            smooth[:, at] = total.T[:ROWS] * gain[0, rows_of(g), at]
        rolled = pltpu.roll(smooth[...], offset[0], 1)
        for chunk in range(4):
            piece = rolled[:, chunk * CHUNK : (chunk + 1) * CHUNK]
            pieces[g, chunk % 2, chunk // 2, pl.ds(0, ROWS), :] = piece
            pieces[g, chunk % 2, chunk // 2, pl.ds(ROWS, META), :] = facts

    def pair(g):
        return pltpu.make_async_remote_copy(
            src_ref=pieces.at[g, 1 - core],
            dst_ref=paired.at[g],
            send_sem=pair_send.at[g],
            recv_sem=pair_recv.at[g],
            device_id={"beam": mate},
            device_id_type=MESH,
        )

    def ring(g, number, peer):
        return pltpu.make_async_remote_copy(
            src_ref=terms.at[g, number],
            dst_ref=landed.at[g, number],
            send_sem=ring_send.at[g, number],
            recv_sem=ring_recv.at[g, number],
            device_id={"beam": peer},
            device_id_type=MESH,
        )

    lane = lax.broadcasted_iota(jnp.int32, (1, CHUNK), 1)

    def term(source, half, which):
        part, late = lax.rem(half, 2), half // 2
        row = (lane + CHUNK * (2 * part + core)).astype(f32)
        told = source[part, pl.ds(ROWS, META), :]
        is_late = jnp.where(row < told[0:1], 1, 0)
        here = (is_late == late) & (told[1:2] == float(which))
        return jnp.where(here, source[part, pl.ds(0, ROWS), :], 0.0)

    def both_terms(g, half, which):
        return term(pieces.at[g, core], half, which) + term(paired.at[g], half, which)

    far, above, below = lax.rem(level + 2, 4), lax.rem(level + 1, 4), lax.rem(level + 3, 4)
    peers = (up, down, up, down, up, down)

    def first_hop(g):
        pair(g).wait_recv()
        for number, half, which in ((0, far, 0), (1, far, 1), (2, above, 1), (3, below, 0)):
            terms[g, number] = both_terms(g, half, which)
            ring(g, number, peers[number]).start()
        terms[g, 4] = both_terms(g, above, 0)
        terms[g, 5] = both_terms(g, below, 1)

    def second_hop(g):
        for number in (0, 1):
            ring(g, number, peers[number]).wait_recv()
            terms[g, 4 + number] += landed[g, number]
            ring(g, 4 + number, peers[4 + number]).start()

    def group(g, carry):
        wait_group(g, tile_recv)
        image_group(g)
        pair(g).start()

        @pl.when(g > 0)
        def _():
            first_hop(g - 1)

        @pl.when(g > 1)
        def _():
            second_hop(g - 2)

        return carry

    lax.fori_loop(0, GROUPS, group, 0)
    first_hop(GROUPS - 1)
    second_hop(GROUPS - 2)
    second_hop(GROUPS - 1)

    def finish(g, carry):
        wait_group(g, tile_send)
        pair(g).wait_send()
        for which in (0, 1):
            total = both_terms(g, level, which)
            for number in (3 - which, 4 + which):
                ring(g, number, peers[number]).wait_recv()
                total += landed[g, number]
            out[which, rows_of(g), :] = total
        for number in range(6):
            ring(g, number, peers[number]).wait_send()
        return carry

    lax.fori_loop(0, GROUPS, finish, 0)


SMEM = pl.BlockSpec(memory_space=pltpu.SMEM)
VMEM = pl.BlockSpec(memory_space=pltpu.VMEM)
ANY = pl.BlockSpec(memory_space=pl.ANY)


def gridded(model, observed, coords, count, block, cell):
    return pl.pallas_call(
        grid_kernel,
        out_shape=jax.ShapeDtypeStruct((NT, SIDE, 2 * SIDE), f32),
        in_specs=[VMEM] * 3 + [SMEM] * 3,
        out_specs=VMEM,
        scratch_shapes=[
            pltpu.VMEM((NT, 2 * SIDE, 2 * SIDE), bf16),
            pltpu.VMEM((SIDE, 2 * SIDE), f32),
            pltpu.VMEM((SIDE, 2 * SIDE), f32),
        ],
        compiler_params=pltpu.CompilerParams(vmem_limit_bytes=VMEM_LIMIT),
        name="grid_residuals",
    )(model, observed, coords, count, block, cell)


def finished(grid, gain, offset, shift, tap_index, taps):
    return pl.pallas_call(
        tail_kernel,
        out_shape=jax.ShapeDtypeStruct((2, SIDE, CHUNK), f32),
        in_specs=[VMEM, ANY] + [SMEM] * 4 + [ANY] * 2,
        out_specs=VMEM,
        scratch_shapes=[
            pltpu.VMEM((NT, 2 * SIDE, 3 * SIDE), bf16),
            pltpu.VMEM((NT, 2 * SIDE, 4 * SIDE), bf16),
            pltpu.VMEM((1, SIDE, G), f32),
            pltpu.VMEM((NT, ROWS, 2 * SIDE), f32),
            pltpu.VMEM((NT, SIDE, 2 * SIDE), f32),
            pltpu.VMEM((NT, SIDE, 2 * SIDE), f32),
            pltpu.VMEM((NT, SIDE, 2 * SIDE), f32),
            pltpu.VMEM((G + 2 * PAD, 2 * SIDE), f32),
            pltpu.VMEM((ROWS, G), f32),
            pltpu.VMEM((GROUPS, 2, 2, ROWS + META, CHUNK), f32),
            pltpu.VMEM((GROUPS, 2, ROWS + META, CHUNK), f32),
            pltpu.VMEM((GROUPS, 6, ROWS, CHUNK), f32),
            pltpu.VMEM((GROUPS, 6, ROWS, CHUNK), f32),
            pltpu.SemaphoreType.DMA((3,)),
            pltpu.SemaphoreType.DMA((GROUPS,)),
            pltpu.SemaphoreType.DMA((GROUPS,)),
            pltpu.SemaphoreType.DMA((GROUPS,)),
            pltpu.SemaphoreType.DMA((GROUPS,)),
            pltpu.SemaphoreType.DMA((GROUPS, 6)),
            pltpu.SemaphoreType.DMA((GROUPS, 6)),
        ],
        compiler_params=pltpu.CompilerParams(
            collective_id=0, has_side_effects=True, vmem_limit_bytes=VMEM_LIMIT
        ),
        name="image_and_sum",
    )(
        grid, gain, offset, shift, tap_index, taps,
        jnp.asarray(row_tables()), jnp.asarray(column_tables()),
    )


def local(
    model_grid, observed, coords, vis_count, subgrid_block, subgrid_cell, beam_gain,
    column_shift, row_offset, interp_index, interp_taps,
):
    grid = gridded(
        model_grid, observed, coords, vis_count, subgrid_block, subgrid_cell,
    )
    return finished(grid, beam_gain, row_offset, column_shift, interp_index, interp_taps)


def solution(mesh):
    placed = (
        P("beam", None, "tile", None),
        P("beam", "tile", None, None),
        P("beam", "tile", None, None),
        P("beam", "tile", None),
        P("beam", "tile", None),
        P("beam", "tile", None),
        P("beam", "tile", None),
        P("beam"),
        P("beam"),
        P("beam", None),
        P(),
    )
    return jax.shard_map(
        local, mesh=mesh, in_specs=placed, out_specs=P(None, "tile", "beam"), check_vma=False
    )
```

```python
import math

import jax
import jax.numpy as jnp
import numpy as np
from jax import lax
from jax.experimental import pallas as pl
from jax.experimental.pallas import tpu as pltpu
from jax.sharding import PartitionSpec as P

SIDE = 64
NT = 32
G = 2048
SLOTS = 256
SUBS = 64
SCALE = 3.0
PAD = 8
BEAMS = 8
CHUNK = 512
GROUPS = 4
ROWS = SIDE // GROUPS
META = 8
VMEM_LIMIT = 56 * 1024 * 1024
MESH = pl.DeviceIdType.MESH

f32 = jnp.float32
bf16 = jnp.bfloat16


def split_np(table):
    high = np.asarray(table, np.float32).astype(bf16)
    low = (np.asarray(table, np.float64) - high.astype(np.float64)).astype(np.float32).astype(bf16)
    return high, low


def row_tables():
    x1 = np.arange(NT)[:, None, None]
    x2 = np.arange(SIDE)[None, :, None]
    w = np.arange(SIDE)[None, None, :]
    angle = 2.0 * math.pi * ((w * (NT * x2 + x1)) % G) / G
    high, low = split_np(np.concatenate([np.cos(angle), np.sin(angle)], axis=1))
    return np.concatenate([high, high, low], axis=2)


def column_tables():
    y1 = np.arange(NT)[:, None, None]
    y2 = np.arange(SIDE)[None, :, None]
    r = np.arange(SIDE)[None, None, :]
    angle = 2.0 * math.pi * ((r * (NT * y2 + y1)) % G) / G
    high, low = split_np(np.concatenate([np.cos(angle), -np.sin(angle)], axis=2) / G)
    top = np.concatenate([high, high], axis=2)
    bottom = np.concatenate([low, np.zeros_like(low)], axis=2)
    return np.concatenate([top, bottom], axis=1)


def split(value):
    high = value.astype(bf16)
    low = (value - high.astype(f32)).astype(bf16)
    return high, low


def lane_signs(shape):
    lane = lax.broadcasted_iota(jnp.int32, shape, 1)
    return jnp.where(lane < SIDE, -1.0, 1.0).astype(f32)


def swapped(value):
    return pltpu.roll(value, SIDE, 1)


def transform(parts, signs):
    n = len(parts)
    if n == 1:
        return parts
    even = transform(parts[0::2], signs)
    odd = transform(parts[1::2], signs)
    low, high = [], []
    for k in range(n // 2):
        if k == 0:
            turned = odd[k]
        elif 4 * k == n:
            turned = swapped(odd[k]) * signs
        else:
            angle = 2.0 * math.pi * k / n
            turned = odd[k] * math.cos(angle) + swapped(odd[k]) * (signs * math.sin(angle))
        low.append(even[k] + turned)
        high.append(even[k] - turned)
    return low + high


def grid_kernel(
    model, observed, coords, count, block, cell, grid, windows, rising, falling
):
    row = lax.broadcasted_iota(jnp.int32, (SIDE, 2 * SIDE), 0).astype(f32)
    rising[...] = jnp.exp(row / SCALE)
    falling[...] = jnp.exp(row / -SCALE)
    left = lax.broadcasted_iota(jnp.int32, (SIDE, 2 * SIDE), 1) < SIDE

    def prepare(pair, carry):
        at = pl.ds(pl.multiple_of(pair * 2 * SIDE, 2 * SIDE), 2 * SIDE)
        for plane in range(2):
            value = model[0, plane, :, at]
            high = value.astype(bf16).astype(f32)
            low = value - high
            rows = pl.ds(plane * SIDE, SIDE)
            windows[2 * pair, rows, :] = jnp.where(left, high, swapped(low)).astype(bf16)
            windows[2 * pair + 1, rows, :] = jnp.where(left, swapped(high), low).astype(bf16)
        return carry

    lax.fori_loop(0, NT // 2, prepare, 0, unroll=8)
    grid[...] = jnp.zeros_like(grid)
    slot = lax.broadcasted_iota(jnp.int32, (2, SLOTS), 1)

    def one(i):
        k = block[0, 0, i]
        q = cell[0, 0, i]
        position = coords[0, k]
        near = jnp.exp(position / -SCALE)
        far = jnp.exp(position / SCALE)
        up = jnp.concatenate([rising[...], rising[...]], axis=1)
        down = jnp.concatenate([falling[...], falling[...]], axis=1)
        along_v = jnp.minimum(up * near[0:1], down * far[0:1])
        along_u = jnp.minimum(up * near[1:2], down * far[1:2])
        high_u, low_u = split(along_u)
        window = windows[q]
        rows = jnp.dot(
            jnp.concatenate([window, window], axis=1),
            jnp.concatenate([high_u, high_u, low_u, low_u], axis=0),
            preferred_element_type=f32,
        )
        predicted = jnp.sum(rows.reshape(2, SIDE, SLOTS) * along_v[None], axis=1)
        residual = jnp.where(slot < count[0, 0, i], observed[0, k] - predicted, 0.0)
        weighted = jnp.concatenate([along_v * residual[0:1], along_v * residual[1:2]], axis=0)
        high_w, low_w = split(weighted.T)
        products = jnp.dot(
            jnp.concatenate([high_u, low_u], axis=0),
            jnp.concatenate([high_w, low_w], axis=1),
            preferred_element_type=f32,
        )
        patch = products[:SIDE, : 2 * SIDE] + (
            products[SIDE:, : 2 * SIDE] + products[:SIDE, 2 * SIDE :]
        )
        return q, patch

    def several(i, carry):
        done = [one(i * 32 + j) for j in range(32)]
        for q, patch in done:
            grid[q] += patch
        return carry

    lax.fori_loop(0, SUBS // 32, several, 0)


def tail_kernel(
    grid, gain_in, offset, shift, tap_index, taps, row_table_in, table_in, out,
    row_table, table, gain, tapped, blocks, landing, spectrum, padded, smooth,
    pieces, paired, terms, landed,
    in_sem, tile_send, tile_recv, pair_send, pair_recv, ring_send, ring_recv,
):
    me = lax.axis_index("tile")
    beam = lax.axis_index("beam")
    level, core = beam // 2, lax.rem(beam, 2)
    mate = beam + 1 - 2 * core
    up, down = lax.rem(beam + 2, BEAMS), lax.rem(beam + 6, BEAMS)
    barrier = pltpu.get_barrier_semaphore()
    for step in range(1, NT):
        pl.semaphore_signal(
            barrier, inc=1, device_id={"tile": lax.rem(me + step, NT)}, device_id_type=MESH
        )
    for peer in (mate, up, down):
        pl.semaphore_signal(barrier, inc=1, device_id={"beam": peer}, device_id_type=MESH)
    row_copy = pltpu.make_async_copy(row_table_in, row_table, in_sem.at[0])
    row_copy.start()
    column_copy = pltpu.make_async_copy(table_in, table, in_sem.at[1])
    column_copy.start()
    gain_copy = pltpu.make_async_copy(gain_in, gain, in_sem.at[2])
    gain_copy.start()

    signs = lane_signs((8, 2 * SIDE))

    def transform_rows(source, start, rows):
        def tile(i, carry):
            at = pl.ds(pl.multiple_of(start + i * 8, 8), 8)
            to = pl.ds(pl.multiple_of(i * 8, 8), 8)
            for k, value in enumerate(transform([source[t, at, :] for t in range(NT)], signs)):
                spectrum[k, to, :] = value
            return carry

        lax.fori_loop(0, rows // 8, tile, 0)

    padded[pl.ds(0, PAD), :] = jnp.zeros((PAD, 2 * SIDE), f32)
    padded[pl.ds(PAD + G, PAD), :] = jnp.zeros((PAD, 2 * SIDE), f32)
    transform_rows(grid, 0, SIDE)
    row_copy.wait()
    wide_signs = lane_signs((SIDE, 2 * SIDE))
    for x1 in range(NT):
        high, low = split(spectrum[x1])
        both = jnp.dot(
            row_table[x1], jnp.concatenate([high, low, high], axis=0), preferred_element_type=f32
        )
        padded[pl.ds(PAD + x1, SIDE, stride=NT), :] = both[:SIDE] + swapped(both[SIDE:]) * wide_signs

    def rows_of(g):
        return pl.ds(pl.multiple_of(g * ROWS, ROWS), ROWS)

    phase_x = tap_index[0, 0]
    weights_x = [taps[phase_x, tap] for tap in range(5)]
    steps = shift[0]

    def make_group(g):
        def make(d, carry):
            start = pl.multiple_of(d * SIDE + g * ROWS, ROWS)
            total = weights_x[0] * padded[pl.ds(start + PAD + 2, ROWS), :]
            for tap in range(1, 5):
                total = total + weights_x[tap] * padded[pl.ds(start + PAD + 2 - tap, ROWS), :]
            tapped[d] = total
            return carry

        def place(d, carry):
            blocks[d, rows_of(g), :] = tapped[lax.rem(d - steps + NT, NT)]
            return carry

        lax.fori_loop(0, NT, make, 0)
        lax.fori_loop(0, NT, place, 0)
        landing[me, rows_of(g), :] = blocks[me, rows_of(g), :]

    def send_group(g):
        def send_one(step, inner):
            peer = lax.rem(me + step, NT)
            pltpu.make_async_remote_copy(
                src_ref=blocks.at[peer, rows_of(g)],
                dst_ref=landing.at[me, rows_of(g)],
                send_sem=tile_send.at[g],
                recv_sem=tile_recv.at[g],
                device_id={"tile": peer},
                device_id_type=MESH,
            ).start()
            return inner

        lax.fori_loop(1, NT, send_one, 0)

    make_group(0)
    pl.semaphore_wait(barrier, NT + 2)

    def start_group(g, carry):
        send_group(g)

        @pl.when(g < GROUPS - 1)
        def _():
            make_group(g + 1)

        return carry

    lax.fori_loop(0, GROUPS, start_group, 0)
    column_copy.wait()
    gain_copy.wait()

    def wait_group(g, semaphores):
        most = pl.ds(0, NT - 1)
        pltpu.make_async_copy(
            blocks.at[most, rows_of(g)], landing.at[most, rows_of(g)], semaphores.at[g]
        ).wait()

    phase = tap_index[0, 1]
    weights = [taps[phase, tap] for tap in range(5)]
    upper = jnp.where(me < shift[0], 1.0, 0.0)
    first = jnp.full((META, CHUNK), offset[0].astype(f32))
    kind = lax.broadcasted_iota(jnp.int32, (META, CHUNK), 0)
    facts = jnp.where(kind == 0, first, upper)

    def image_group(g):
        transform_rows(landing, g * ROWS, ROWS)
        for y1 in range(NT):
            high, low = split(spectrum[y1, pl.ds(0, ROWS), :])
            both = lax.dot_general(
                table[y1],
                jnp.concatenate([high, low], axis=1),
                (((1,), (1,)), ((), ())),
                preferred_element_type=f32,
            )
            padded[pl.ds(PAD + y1, SIDE, stride=NT), pl.ds(0, ROWS)] = both[:SIDE] + both[SIDE:]
        for part in range(G // 128):
            total = weights[0] * padded[pl.ds(part * 128 + PAD + 2, 128), :]
            for tap in range(1, 5):
                total = total + weights[tap] * padded[pl.ds(part * 128 + PAD + 2 - tap, 128), :]
            at = pl.ds(part * 128, 128)
            smooth[:, at] = total.T[:ROWS] * gain[0, rows_of(g), at]
        rolled = pltpu.roll(smooth[...], offset[0], 1)
        for chunk in range(4):
            piece = rolled[:, chunk * CHUNK : (chunk + 1) * CHUNK]
            pieces[g, chunk % 2, chunk // 2, pl.ds(0, ROWS), :] = piece
            pieces[g, chunk % 2, chunk // 2, pl.ds(ROWS, META), :] = facts

    def pair(g):
        return pltpu.make_async_remote_copy(
            src_ref=pieces.at[g, 1 - core],
            dst_ref=paired.at[g],
            send_sem=pair_send.at[g],
            recv_sem=pair_recv.at[g],
            device_id={"beam": mate},
            device_id_type=MESH,
        )

    def ring(g, number, peer):
        return pltpu.make_async_remote_copy(
            src_ref=terms.at[g, number],
            dst_ref=landed.at[g, number],
            send_sem=ring_send.at[g, number],
            recv_sem=ring_recv.at[g, number],
            device_id={"beam": peer},
            device_id_type=MESH,
        )

    lane = lax.broadcasted_iota(jnp.int32, (1, CHUNK), 1)

    def term(source, half, which):
        part, late = lax.rem(half, 2), half // 2
        row = (lane + CHUNK * (2 * part + core)).astype(f32)
        told = source[part, pl.ds(ROWS, META), :]
        is_late = jnp.where(row < told[0:1], 1, 0)
        here = (is_late == late) & (told[1:2] == float(which))
        return jnp.where(here, source[part, pl.ds(0, ROWS), :], 0.0)

    def both_terms(g, half, which):
        return term(pieces.at[g, core], half, which) + term(paired.at[g], half, which)

    far, above, below = lax.rem(level + 2, 4), lax.rem(level + 1, 4), lax.rem(level + 3, 4)
    peers = (up, down, up, down, up, down)

    def first_hop(g):
        pair(g).wait_recv()
        for number, half, which in ((0, far, 0), (1, far, 1), (2, above, 1), (3, below, 0)):
            terms[g, number] = both_terms(g, half, which)
            ring(g, number, peers[number]).start()
        terms[g, 4] = both_terms(g, above, 0)
        terms[g, 5] = both_terms(g, below, 1)

    def second_hop(g):
        for number in (0, 1):
            ring(g, number, peers[number]).wait_recv()
            terms[g, 4 + number] += landed[g, number]
            ring(g, 4 + number, peers[4 + number]).start()

    def group(g, carry):
        wait_group(g, tile_recv)
        image_group(g)
        pair(g).start()

        @pl.when(g > 0)
        def _():
            first_hop(g - 1)

        @pl.when(g > 1)
        def _():
            second_hop(g - 2)

        return carry

    lax.fori_loop(0, GROUPS, group, 0)
    first_hop(GROUPS - 1)
    second_hop(GROUPS - 2)
    second_hop(GROUPS - 1)

    def finish(g, carry):
        wait_group(g, tile_send)
        pair(g).wait_send()
        for which in (0, 1):
            total = both_terms(g, level, which)
            for number in (3 - which, 4 + which):
                ring(g, number, peers[number]).wait_recv()
                total += landed[g, number]
            out[which, rows_of(g), :] = total
        for number in range(6):
            ring(g, number, peers[number]).wait_send()
        return carry

    lax.fori_loop(0, GROUPS, finish, 0)


SMEM = pl.BlockSpec(memory_space=pltpu.SMEM)
VMEM = pl.BlockSpec(memory_space=pltpu.VMEM)
ANY = pl.BlockSpec(memory_space=pl.ANY)


def gridded(model, observed, coords, count, block, cell):
    return pl.pallas_call(
        grid_kernel,
        out_shape=jax.ShapeDtypeStruct((NT, SIDE, 2 * SIDE), f32),
        in_specs=[VMEM] * 3 + [SMEM] * 3,
        out_specs=VMEM,
        scratch_shapes=[
            pltpu.VMEM((NT, 2 * SIDE, 2 * SIDE), bf16),
            pltpu.VMEM((SIDE, 2 * SIDE), f32),
            pltpu.VMEM((SIDE, 2 * SIDE), f32),
        ],
        compiler_params=pltpu.CompilerParams(vmem_limit_bytes=VMEM_LIMIT),
        name="grid_residuals",
    )(model, observed, coords, count, block, cell)


def finished(grid, gain, offset, shift, tap_index, taps):
    return pl.pallas_call(
        tail_kernel,
        out_shape=jax.ShapeDtypeStruct((2, SIDE, CHUNK), f32),
        in_specs=[VMEM, ANY] + [SMEM] * 4 + [ANY] * 2,
        out_specs=VMEM,
        scratch_shapes=[
            pltpu.VMEM((NT, 2 * SIDE, 3 * SIDE), bf16),
            pltpu.VMEM((NT, 2 * SIDE, 4 * SIDE), bf16),
            pltpu.VMEM((1, SIDE, G), f32),
            pltpu.VMEM((NT, ROWS, 2 * SIDE), f32),
            pltpu.VMEM((NT, SIDE, 2 * SIDE), f32),
            pltpu.VMEM((NT, SIDE, 2 * SIDE), f32),
            pltpu.VMEM((NT, SIDE, 2 * SIDE), f32),
            pltpu.VMEM((G + 2 * PAD, 2 * SIDE), f32),
            pltpu.VMEM((ROWS, G), f32),
            pltpu.VMEM((GROUPS, 2, 2, ROWS + META, CHUNK), f32),
            pltpu.VMEM((GROUPS, 2, ROWS + META, CHUNK), f32),
            pltpu.VMEM((GROUPS, 6, ROWS, CHUNK), f32),
            pltpu.VMEM((GROUPS, 6, ROWS, CHUNK), f32),
            pltpu.SemaphoreType.DMA((3,)),
            pltpu.SemaphoreType.DMA((GROUPS,)),
            pltpu.SemaphoreType.DMA((GROUPS,)),
            pltpu.SemaphoreType.DMA((GROUPS,)),
            pltpu.SemaphoreType.DMA((GROUPS,)),
            pltpu.SemaphoreType.DMA((GROUPS, 6)),
            pltpu.SemaphoreType.DMA((GROUPS, 6)),
        ],
        compiler_params=pltpu.CompilerParams(
            collective_id=0, has_side_effects=True, vmem_limit_bytes=VMEM_LIMIT
        ),
        name="image_and_sum",
    )(
        grid, gain, offset, shift, tap_index, taps,
        jnp.asarray(row_tables()), jnp.asarray(column_tables()),
    )


def local(
    model_grid, observed, coords, vis_count, subgrid_block, subgrid_cell, beam_gain,
    column_shift, row_offset, interp_index, interp_taps,
):
    grid = gridded(
        model_grid, observed, coords, vis_count, subgrid_block, subgrid_cell,
    )
    return finished(grid, beam_gain, row_offset, column_shift, interp_index, interp_taps)


def solution(mesh):
    placed = (
        P("beam", None, "tile", None),
        P("beam", "tile", None, None),
        P("beam", "tile", None, None),
        P("beam", "tile", None),
        P("beam", "tile", None),
        P("beam", "tile", None),
        P("beam", "tile", None),
        P("beam"),
        P("beam"),
        P("beam", None),
        P(),
    )
    return jax.shard_map(
        local, mesh=mesh, in_specs=placed, out_specs=P(None, "tile", "beam"), check_vma=False
    )
```

```python
import math

import jax
import jax.numpy as jnp
import numpy as np
from jax import lax
from jax.experimental import pallas as pl
from jax.experimental.pallas import tpu as pltpu
from jax.sharding import PartitionSpec as P

SIDE = 64
NT = 32
G = 2048
SLOTS = 256
SUBS = 64
SCALE = 3.0
PAD = 8
BEAMS = 8
CHUNK = 512
GROUPS = 4
ROWS = SIDE // GROUPS
META = 8
VMEM_LIMIT = 56 * 1024 * 1024
MESH = pl.DeviceIdType.MESH

f32 = jnp.float32
bf16 = jnp.bfloat16


def split_np(table):
    high = np.asarray(table, np.float32).astype(bf16)
    low = (np.asarray(table, np.float64) - high.astype(np.float64)).astype(np.float32).astype(bf16)
    return high, low


def row_tables():
    x1 = np.arange(NT)[:, None, None]
    x2 = np.arange(SIDE)[None, :, None]
    w = np.arange(SIDE)[None, None, :]
    angle = 2.0 * math.pi * ((w * (NT * x2 + x1)) % G) / G
    high, low = split_np(np.concatenate([np.cos(angle), np.sin(angle)], axis=1))
    return np.concatenate([high, high, low], axis=2)


def column_tables():
    y1 = np.arange(NT)[:, None, None]
    y2 = np.arange(SIDE)[None, :, None]
    r = np.arange(SIDE)[None, None, :]
    angle = 2.0 * math.pi * ((r * (NT * y2 + y1)) % G) / G
    high, low = split_np(np.concatenate([np.cos(angle), -np.sin(angle)], axis=2) / G)
    top = np.concatenate([high, high], axis=2)
    bottom = np.concatenate([low, np.zeros_like(low)], axis=2)
    return np.concatenate([top, bottom], axis=1)


def split(value):
    high = value.astype(bf16)
    low = (value - high.astype(f32)).astype(bf16)
    return high, low


def lane_signs(shape):
    lane = lax.broadcasted_iota(jnp.int32, shape, 1)
    return jnp.where(lane < SIDE, -1.0, 1.0).astype(f32)


def swapped(value):
    return pltpu.roll(value, SIDE, 1)


def transform(parts, signs):
    n = len(parts)
    if n == 1:
        return parts
    even = transform(parts[0::2], signs)
    odd = transform(parts[1::2], signs)
    low, high = [], []
    for k in range(n // 2):
        if k == 0:
            turned = odd[k]
        elif 4 * k == n:
            turned = swapped(odd[k]) * signs
        else:
            angle = 2.0 * math.pi * k / n
            turned = odd[k] * math.cos(angle) + swapped(odd[k]) * (signs * math.sin(angle))
        low.append(even[k] + turned)
        high.append(even[k] - turned)
    return low + high


def grid_kernel(
    model, observed, coords, count, block, cell, grid, windows, rising, falling
):
    row = lax.broadcasted_iota(jnp.int32, (SIDE, 2 * SIDE), 0).astype(f32)
    rising[...] = jnp.exp(row / SCALE)
    falling[...] = jnp.exp(row / -SCALE)
    left = lax.broadcasted_iota(jnp.int32, (SIDE, 2 * SIDE), 1) < SIDE

    def prepare(pair, carry):
        at = pl.ds(pl.multiple_of(pair * 2 * SIDE, 2 * SIDE), 2 * SIDE)
        for plane in range(2):
            value = model[0, plane, :, at]
            high = value.astype(bf16).astype(f32)
            low = value - high
            rows = pl.ds(plane * SIDE, SIDE)
            windows[2 * pair, rows, :] = jnp.where(left, high, swapped(low)).astype(bf16)
            windows[2 * pair + 1, rows, :] = jnp.where(left, swapped(high), low).astype(bf16)
        return carry

    lax.fori_loop(0, NT // 2, prepare, 0, unroll=8)
    grid[...] = jnp.zeros_like(grid)
    slot = lax.broadcasted_iota(jnp.int32, (2, SLOTS), 1)

    def one(i):
        k = block[0, 0, i]
        q = cell[0, 0, i]
        position = coords[0, k]
        near = jnp.exp(position / -SCALE)
        far = jnp.exp(position / SCALE)
        up = jnp.concatenate([rising[...], rising[...]], axis=1)
        down = jnp.concatenate([falling[...], falling[...]], axis=1)
        along_v = jnp.minimum(up * near[0:1], down * far[0:1])
        along_u = jnp.minimum(up * near[1:2], down * far[1:2])
        high_u, low_u = split(along_u)
        window = windows[q]
        rows = jnp.dot(
            jnp.concatenate([window, window], axis=1),
            jnp.concatenate([high_u, high_u, low_u, low_u], axis=0),
            preferred_element_type=f32,
        )
        predicted = jnp.sum(rows.reshape(2, SIDE, SLOTS) * along_v[None], axis=1)
        residual = jnp.where(slot < count[0, 0, i], observed[0, k] - predicted, 0.0)
        weighted = jnp.concatenate([along_v * residual[0:1], along_v * residual[1:2]], axis=0)
        high_w, low_w = split(weighted.T)
        products = jnp.dot(
            jnp.concatenate([high_u, low_u], axis=0),
            jnp.concatenate([high_w, low_w], axis=1),
            preferred_element_type=f32,
        )
        patch = products[:SIDE, : 2 * SIDE] + (
            products[SIDE:, : 2 * SIDE] + products[:SIDE, 2 * SIDE :]
        )
        return q, patch

    def several(i, carry):
        done = [one(i * 32 + j) for j in range(32)]
        for q, patch in done:
            grid[q] += patch
        return carry

    lax.fori_loop(0, SUBS // 32, several, 0)


def tail_kernel(
    grid, gain_in, offset, shift, tap_index, taps, row_table_in, table_in, out,
    row_table, table, gain, tapped, blocks, landing, spectrum, padded, smooth,
    pieces, paired, terms, landed,
    in_sem, tile_send, tile_recv, pair_send, pair_recv, ring_send, ring_recv,
):
    me = lax.axis_index("tile")
    beam = lax.axis_index("beam")
    level, core = beam // 2, lax.rem(beam, 2)
    mate = beam + 1 - 2 * core
    up, down = lax.rem(beam + 2, BEAMS), lax.rem(beam + 6, BEAMS)
    barrier = pltpu.get_barrier_semaphore()
    for step in range(1, NT):
        pl.semaphore_signal(
            barrier, inc=1, device_id={"tile": lax.rem(me + step, NT)}, device_id_type=MESH
        )
    for peer in (mate, up, down):
        pl.semaphore_signal(barrier, inc=1, device_id={"beam": peer}, device_id_type=MESH)
    row_copy = pltpu.make_async_copy(row_table_in, row_table, in_sem.at[0])
    row_copy.start()
    column_copy = pltpu.make_async_copy(table_in, table, in_sem.at[1])
    column_copy.start()
    gain_copy = pltpu.make_async_copy(gain_in, gain, in_sem.at[2])
    gain_copy.start()

    signs = lane_signs((8, 2 * SIDE))

    def transform_rows(source, start, rows):
        def tile(i, carry):
            at = pl.ds(pl.multiple_of(start + i * 8, 8), 8)
            to = pl.ds(pl.multiple_of(i * 8, 8), 8)
            for k, value in enumerate(transform([source[t, at, :] for t in range(NT)], signs)):
                spectrum[k, to, :] = value
            return carry

        lax.fori_loop(0, rows // 8, tile, 0)

    padded[pl.ds(0, PAD), :] = jnp.zeros((PAD, 2 * SIDE), f32)
    padded[pl.ds(PAD + G, PAD), :] = jnp.zeros((PAD, 2 * SIDE), f32)
    transform_rows(grid, 0, SIDE)
    row_copy.wait()
    wide_signs = lane_signs((SIDE, 2 * SIDE))
    for x1 in range(NT):
        high, low = split(spectrum[x1])
        both = jnp.dot(
            row_table[x1], jnp.concatenate([high, low, high], axis=0), preferred_element_type=f32
        )
        padded[pl.ds(PAD + x1, SIDE, stride=NT), :] = both[:SIDE] + swapped(both[SIDE:]) * wide_signs

    def rows_of(g):
        return pl.ds(pl.multiple_of(g * ROWS, ROWS), ROWS)

    phase_x = tap_index[0, 0]
    weights_x = [taps[phase_x, tap] for tap in range(5)]
    steps = shift[0]

    def make_group(g):
        def make(d, carry):
            start = pl.multiple_of(d * SIDE + g * ROWS, ROWS)
            total = weights_x[0] * padded[pl.ds(start + PAD + 2, ROWS), :]
            for tap in range(1, 5):
                total = total + weights_x[tap] * padded[pl.ds(start + PAD + 2 - tap, ROWS), :]
            tapped[d] = total
            return carry

        def place(d, carry):
            blocks[d, rows_of(g), :] = tapped[lax.rem(d - steps + NT, NT)]
            return carry

        lax.fori_loop(0, NT, make, 0, unroll=8)
        lax.fori_loop(0, NT, place, 0, unroll=8)
        landing[me, rows_of(g), :] = blocks[me, rows_of(g), :]

    side, place_xy = me // 16, lax.rem(me, 16)

    def peer_of(step):
        return lax.rem(side + 1 + step, 2) * 16 + lax.rem(place_xy + step // 2, 16)

    def send_group(g):
        def send_one(step, inner):
            peer = peer_of(step)
            pltpu.make_async_remote_copy(
                src_ref=blocks.at[peer, rows_of(g)],
                dst_ref=landing.at[me, rows_of(g)],
                send_sem=tile_send.at[g],
                recv_sem=tile_recv.at[g],
                device_id={"tile": peer},
                device_id_type=MESH,
            ).start()
            return inner

        send_one(0, 0)
        lax.fori_loop(2, NT, send_one, 0)

    make_group(0)
    pl.semaphore_wait(barrier, NT + 2)

    def start_group(g, carry):
        send_group(g)

        @pl.when(g < GROUPS - 1)
        def _():
            make_group(g + 1)

        return carry

    lax.fori_loop(0, GROUPS, start_group, 0)
    column_copy.wait()
    gain_copy.wait()

    def wait_group(g, semaphores):
        most = pl.ds(0, NT - 1)
        pltpu.make_async_copy(
            blocks.at[most, rows_of(g)], landing.at[most, rows_of(g)], semaphores.at[g]
        ).wait()

    phase = tap_index[0, 1]
    weights = [taps[phase, tap] for tap in range(5)]
    upper = jnp.where(me < shift[0], 1.0, 0.0)
    first = jnp.full((META, CHUNK), offset[0].astype(f32))
    kind = lax.broadcasted_iota(jnp.int32, (META, CHUNK), 0)
    facts = jnp.where(kind == 0, first, upper)

    def image_group(g):
        transform_rows(landing, g * ROWS, ROWS)
        for y1 in range(NT):
            high, low = split(spectrum[y1, pl.ds(0, ROWS), :])
            both = lax.dot_general(
                table[y1],
                jnp.concatenate([high, low], axis=1),
                (((1,), (1,)), ((), ())),
                preferred_element_type=f32,
            )
            padded[pl.ds(PAD + y1, SIDE, stride=NT), pl.ds(0, ROWS)] = both[:SIDE] + both[SIDE:]
        for part in range(G // 128):
            total = weights[0] * padded[pl.ds(part * 128 + PAD + 2, 128), :]
            for tap in range(1, 5):
                total = total + weights[tap] * padded[pl.ds(part * 128 + PAD + 2 - tap, 128), :]
            at = pl.ds(part * 128, 128)
            smooth[:, at] = total.T[:ROWS] * gain[0, rows_of(g), at]
        rolled = pltpu.roll(smooth[...], offset[0], 1)
        for chunk in range(4):
            piece = rolled[:, chunk * CHUNK : (chunk + 1) * CHUNK]
            pieces[g, chunk % 2, chunk // 2, pl.ds(0, ROWS), :] = piece
            pieces[g, chunk % 2, chunk // 2, pl.ds(ROWS, META), :] = facts

    def pair(g):
        return pltpu.make_async_remote_copy(
            src_ref=pieces.at[g, 1 - core],
            dst_ref=paired.at[g],
            send_sem=pair_send.at[g],
            recv_sem=pair_recv.at[g],
            device_id={"beam": mate},
            device_id_type=MESH,
        )

    def ring(g, number, peer):
        return pltpu.make_async_remote_copy(
            src_ref=terms.at[g, number],
            dst_ref=landed.at[g, number],
            send_sem=ring_send.at[g, number],
            recv_sem=ring_recv.at[g, number],
            device_id={"beam": peer},
            device_id_type=MESH,
        )

    lane = lax.broadcasted_iota(jnp.int32, (1, CHUNK), 1)

    def term(source, half, which):
        part, late = lax.rem(half, 2), half // 2
        row = (lane + CHUNK * (2 * part + core)).astype(f32)
        told = source[part, pl.ds(ROWS, META), :]
        is_late = jnp.where(row < told[0:1], 1, 0)
        here = (is_late == late) & (told[1:2] == float(which))
        return jnp.where(here, source[part, pl.ds(0, ROWS), :], 0.0)

    def both_terms(g, half, which):
        return term(pieces.at[g, core], half, which) + term(paired.at[g], half, which)

    far, above, below = lax.rem(level + 2, 4), lax.rem(level + 1, 4), lax.rem(level + 3, 4)
    peers = (up, down, up, down, up, down)

    def first_hop(g):
        pair(g).wait_recv()
        for number, half, which in ((0, far, 0), (1, far, 1), (2, above, 1), (3, below, 0)):
            terms[g, number] = both_terms(g, half, which)
            ring(g, number, peers[number]).start()
        terms[g, 4] = both_terms(g, above, 0)
        terms[g, 5] = both_terms(g, below, 1)

    def second_hop(g):
        for number in (0, 1):
            ring(g, number, peers[number]).wait_recv()
            terms[g, 4 + number] += landed[g, number]
            ring(g, 4 + number, peers[4 + number]).start()

    def group(g, carry):
        wait_group(g, tile_recv)
        image_group(g)
        pair(g).start()

        @pl.when(g > 0)
        def _():
            first_hop(g - 1)

        @pl.when(g > 1)
        def _():
            second_hop(g - 2)

        return carry

    lax.fori_loop(0, GROUPS, group, 0)
    first_hop(GROUPS - 1)
    second_hop(GROUPS - 2)
    second_hop(GROUPS - 1)

    def finish(g, carry):
        wait_group(g, tile_send)
        pair(g).wait_send()
        for which in (0, 1):
            total = both_terms(g, level, which)
            for number in (3 - which, 4 + which):
                ring(g, number, peers[number]).wait_recv()
                total += landed[g, number]
            out[which, rows_of(g), :] = total
        for number in range(6):
            ring(g, number, peers[number]).wait_send()
        return carry

    lax.fori_loop(0, GROUPS, finish, 0)


SMEM = pl.BlockSpec(memory_space=pltpu.SMEM)
VMEM = pl.BlockSpec(memory_space=pltpu.VMEM)
ANY = pl.BlockSpec(memory_space=pl.ANY)


def gridded(model, observed, coords, count, block, cell):
    return pl.pallas_call(
        grid_kernel,
        out_shape=pltpu.VMEM((NT, SIDE, 2 * SIDE), f32),
        in_specs=[VMEM] * 3 + [SMEM] * 3,
        out_specs=VMEM,
        scratch_shapes=[
            pltpu.VMEM((NT, 2 * SIDE, 2 * SIDE), bf16),
            pltpu.VMEM((SIDE, 2 * SIDE), f32),
            pltpu.VMEM((SIDE, 2 * SIDE), f32),
        ],
        compiler_params=pltpu.CompilerParams(vmem_limit_bytes=VMEM_LIMIT),
        name="grid_residuals",
    )(model, observed, coords, count, block, cell)


def finished(grid, gain, offset, shift, tap_index, taps):
    return pl.pallas_call(
        tail_kernel,
        out_shape=pltpu.VMEM((2, SIDE, CHUNK), f32),
        in_specs=[VMEM, ANY] + [SMEM] * 4 + [ANY] * 2,
        out_specs=VMEM,
        scratch_shapes=[
            pltpu.VMEM((NT, 2 * SIDE, 3 * SIDE), bf16),
            pltpu.VMEM((NT, 2 * SIDE, 4 * SIDE), bf16),
            pltpu.VMEM((1, SIDE, G), f32),
            pltpu.VMEM((NT, ROWS, 2 * SIDE), f32),
            pltpu.VMEM((NT, SIDE, 2 * SIDE), f32),
            pltpu.VMEM((NT, SIDE, 2 * SIDE), f32),
            pltpu.VMEM((NT, SIDE, 2 * SIDE), f32),
            pltpu.VMEM((G + 2 * PAD, 2 * SIDE), f32),
            pltpu.VMEM((ROWS, G), f32),
            pltpu.VMEM((GROUPS, 2, 2, ROWS + META, CHUNK), f32),
            pltpu.VMEM((GROUPS, 2, ROWS + META, CHUNK), f32),
            pltpu.VMEM((GROUPS, 6, ROWS, CHUNK), f32),
            pltpu.VMEM((GROUPS, 6, ROWS, CHUNK), f32),
            pltpu.SemaphoreType.DMA((3,)),
            pltpu.SemaphoreType.DMA((GROUPS,)),
            pltpu.SemaphoreType.DMA((GROUPS,)),
            pltpu.SemaphoreType.DMA((GROUPS,)),
            pltpu.SemaphoreType.DMA((GROUPS,)),
            pltpu.SemaphoreType.DMA((GROUPS, 6)),
            pltpu.SemaphoreType.DMA((GROUPS, 6)),
        ],
        compiler_params=pltpu.CompilerParams(
            collective_id=0, has_side_effects=True, vmem_limit_bytes=VMEM_LIMIT
        ),
        name="image_and_sum",
    )(
        grid, gain, offset, shift, tap_index, taps,
        jnp.asarray(row_tables()), jnp.asarray(column_tables()),
    )


def local(
    model_grid, observed, coords, vis_count, subgrid_block, subgrid_cell, beam_gain,
    column_shift, row_offset, interp_index, interp_taps,
):
    grid = gridded(
        model_grid, observed, coords, vis_count, subgrid_block, subgrid_cell,
    )
    grid = pltpu.with_memory_space_constraint(grid, pltpu.VMEM)
    return finished(grid, beam_gain, row_offset, column_shift, interp_index, interp_taps)


def solution(mesh):
    placed = (
        P("beam", None, "tile", None),
        P("beam", "tile", None, None),
        P("beam", "tile", None, None),
        P("beam", "tile", None),
        P("beam", "tile", None),
        P("beam", "tile", None),
        P("beam", "tile", None),
        P("beam"),
        P("beam"),
        P("beam", None),
        P(),
    )
    return jax.shard_map(
        local, mesh=mesh, in_specs=placed, out_specs=P(None, "tile", "beam"), check_vma=False
    )
```

```python
import math

import jax
import jax.numpy as jnp
import numpy as np
from jax import lax
from jax.experimental import pallas as pl
from jax.experimental.pallas import tpu as pltpu
from jax.sharding import PartitionSpec as P

SIDE = 64
NT = 32
G = 2048
SLOTS = 256
SUBS = 64
SCALE = 3.0
PAD = 8
BEAMS = 8
CHUNK = 512
GROUPS = 4
ROWS = SIDE // GROUPS
META = 8
VMEM_LIMIT = 56 * 1024 * 1024
MESH = pl.DeviceIdType.MESH

f32 = jnp.float32
bf16 = jnp.bfloat16


def split_np(table):
    high = np.asarray(table, np.float32).astype(bf16)
    low = (np.asarray(table, np.float64) - high.astype(np.float64)).astype(np.float32).astype(bf16)
    return high, low


def row_tables():
    x1 = np.arange(NT)[:, None, None]
    x2 = np.arange(SIDE)[None, :, None]
    w = np.arange(SIDE)[None, None, :]
    angle = 2.0 * math.pi * ((w * (NT * x2 + x1)) % G) / G
    high, low = split_np(np.concatenate([np.cos(angle), np.sin(angle)], axis=1))
    return np.concatenate([high, high, low], axis=2)


def column_tables():
    y1 = np.arange(NT)[:, None, None]
    y2 = np.arange(SIDE)[None, :, None]
    r = np.arange(SIDE)[None, None, :]
    angle = 2.0 * math.pi * ((r * (NT * y2 + y1)) % G) / G
    high, low = split_np(np.concatenate([np.cos(angle), -np.sin(angle)], axis=2) / G)
    top = np.concatenate([high, high], axis=2)
    bottom = np.concatenate([low, np.zeros_like(low)], axis=2)
    return np.concatenate([top, bottom], axis=1)


def split(value):
    high = value.astype(bf16)
    low = (value - high.astype(f32)).astype(bf16)
    return high, low


def lane_signs(shape):
    lane = lax.broadcasted_iota(jnp.int32, shape, 1)
    return jnp.where(lane < SIDE, -1.0, 1.0).astype(f32)


def swapped(value):
    return pltpu.roll(value, SIDE, 1)


def transform(parts, signs):
    n = len(parts)
    if n == 1:
        return parts
    even = transform(parts[0::2], signs)
    odd = transform(parts[1::2], signs)
    low, high = [], []
    for k in range(n // 2):
        if k == 0:
            turned = odd[k]
        elif 4 * k == n:
            turned = swapped(odd[k]) * signs
        else:
            angle = 2.0 * math.pi * k / n
            turned = odd[k] * math.cos(angle) + swapped(odd[k]) * (signs * math.sin(angle))
        low.append(even[k] + turned)
        high.append(even[k] - turned)
    return low + high


def grid_kernel(
    model, observed, coords, count, block, cell, grid, windows, rising, falling
):
    row = lax.broadcasted_iota(jnp.int32, (SIDE, 2 * SIDE), 0).astype(f32)
    rising[...] = jnp.exp(row / SCALE)
    falling[...] = jnp.exp(row / -SCALE)
    left = lax.broadcasted_iota(jnp.int32, (SIDE, 2 * SIDE), 1) < SIDE

    def prepare(pair, carry):
        at = pl.ds(pl.multiple_of(pair * 2 * SIDE, 2 * SIDE), 2 * SIDE)
        for plane in range(2):
            value = model[0, plane, :, at]
            high = value.astype(bf16).astype(f32)
            low = value - high
            rows = pl.ds(plane * SIDE, SIDE)
            windows[2 * pair, rows, :] = jnp.where(left, high, swapped(low)).astype(bf16)
            windows[2 * pair + 1, rows, :] = jnp.where(left, swapped(high), low).astype(bf16)
        return carry

    lax.fori_loop(0, NT // 2, prepare, 0, unroll=8)
    grid[...] = jnp.zeros_like(grid)
    slot = lax.broadcasted_iota(jnp.int32, (2, SLOTS), 1)

    def one(i):
        k = block[0, 0, i]
        q = cell[0, 0, i]
        position = coords[0, k]
        near = jnp.exp(position / -SCALE)
        far = jnp.exp(position / SCALE)
        up = jnp.concatenate([rising[...], rising[...]], axis=1)
        down = jnp.concatenate([falling[...], falling[...]], axis=1)
        along_v = jnp.minimum(up * near[0:1], down * far[0:1])
        along_u = jnp.minimum(up * near[1:2], down * far[1:2])
        high_u, low_u = split(along_u)
        window = windows[q]
        rows = jnp.dot(
            jnp.concatenate([window, window], axis=1),
            jnp.concatenate([high_u, high_u, low_u, low_u], axis=0),
            preferred_element_type=f32,
        )
        predicted = jnp.sum(rows.reshape(2, SIDE, SLOTS) * along_v[None], axis=1)
        residual = jnp.where(slot < count[0, 0, i], observed[0, k] - predicted, 0.0)
        weighted = jnp.concatenate([along_v * residual[0:1], along_v * residual[1:2]], axis=0)
        high_w, low_w = split(weighted.T)
        products = jnp.dot(
            jnp.concatenate([high_u, low_u], axis=0),
            jnp.concatenate([high_w, low_w], axis=1),
            preferred_element_type=f32,
        )
        patch = products[:SIDE, : 2 * SIDE] + (
            products[SIDE:, : 2 * SIDE] + products[:SIDE, 2 * SIDE :]
        )
        return q, patch

    def several(i, carry):
        done = [one(i * 32 + j) for j in range(32)]
        for q, patch in done:
            grid[q] += patch
        return carry

    lax.fori_loop(0, SUBS // 32, several, 0)


def tail_kernel(
    grid, gain_in, offset, shift, tap_index, taps, row_table_in, table_in, out,
    row_table, table, gain, tapped, blocks, landing, spectrum, padded, smooth,
    pieces, paired, terms, landed,
    in_sem, tile_send, tile_recv, pair_send, pair_recv, ring_send, ring_recv,
):
    me = lax.axis_index("tile")
    beam = lax.axis_index("beam")
    level, core = beam // 2, lax.rem(beam, 2)
    mate = beam + 1 - 2 * core
    up, down = lax.rem(beam + 2, BEAMS), lax.rem(beam + 6, BEAMS)
    barrier = pltpu.get_barrier_semaphore()
    for step in range(1, NT):
        pl.semaphore_signal(
            barrier, inc=1, device_id={"tile": lax.rem(me + step, NT)}, device_id_type=MESH
        )
    for peer in (mate, up, down):
        pl.semaphore_signal(barrier, inc=1, device_id={"beam": peer}, device_id_type=MESH)
    row_copy = pltpu.make_async_copy(row_table_in, row_table, in_sem.at[0])
    row_copy.start()
    column_copy = pltpu.make_async_copy(table_in, table, in_sem.at[1])
    column_copy.start()
    gain_copy = pltpu.make_async_copy(gain_in, gain, in_sem.at[2])
    gain_copy.start()

    signs = lane_signs((8, 2 * SIDE))

    def transform_rows(source, start, rows):
        def tile(i, carry):
            at = pl.ds(pl.multiple_of(start + i * 8, 8), 8)
            to = pl.ds(pl.multiple_of(i * 8, 8), 8)
            for k, value in enumerate(transform([source[t, at, :] for t in range(NT)], signs)):
                spectrum[k, to, :] = value
            return carry

        lax.fori_loop(0, rows // 8, tile, 0, unroll=4 if rows > 32 else 2)

    padded[pl.ds(0, PAD), :] = jnp.zeros((PAD, 2 * SIDE), f32)
    padded[pl.ds(PAD + G, PAD), :] = jnp.zeros((PAD, 2 * SIDE), f32)
    transform_rows(grid, 0, SIDE)
    row_copy.wait()
    wide_signs = lane_signs((SIDE, 2 * SIDE))

    def row_step(x1):
        high, low = split(spectrum[x1])
        both = jnp.dot(
            row_table[x1], jnp.concatenate([high, low, high], axis=0), preferred_element_type=f32
        )
        padded[pl.ds(PAD + x1, SIDE, stride=NT), :] = both[:SIDE] + swapped(both[SIDE:]) * wide_signs

    def first_row(g):
        return pl.multiple_of((lax.rem(g, 2) * 2 + g // 2) * ROWS, ROWS)

    def rows_of(g):
        return pl.ds(first_row(g), ROWS)

    phase_x = tap_index[0, 0]
    weights_x = [taps[phase_x, tap] for tap in range(5)]
    steps = shift[0]

    def make_group(g):
        def make(d, carry):
            start = pl.multiple_of(d * SIDE + first_row(g), ROWS)
            total = weights_x[0] * padded[pl.ds(start + PAD + 2, ROWS), :]
            for tap in range(1, 5):
                total = total + weights_x[tap] * padded[pl.ds(start + PAD + 2 - tap, ROWS), :]
            tapped[d] = total
            return carry

        def place(d, carry):
            blocks[d, rows_of(g), :] = tapped[lax.rem(d - steps + NT, NT)]
            return carry

        lax.fori_loop(0, NT, make, 0, unroll=8)
        lax.fori_loop(0, NT, place, 0, unroll=8)
        landing[me, rows_of(g), :] = blocks[me, rows_of(g), :]

    side, place_xy = me // 16, lax.rem(me, 16)

    def peer_of(step):
        return lax.rem(side + 1 + step, 2) * 16 + lax.rem(place_xy + step // 2, 16)

    def send_group(g):
        def send_one(step, inner):
            peer = peer_of(step)
            pltpu.make_async_remote_copy(
                src_ref=blocks.at[peer, rows_of(g)],
                dst_ref=landing.at[me, rows_of(g)],
                send_sem=tile_send.at[g],
                recv_sem=tile_recv.at[g],
                device_id={"tile": peer},
                device_id_type=MESH,
            ).start()
            return inner

        send_one(0, 0)
        lax.fori_loop(2, NT, send_one, 0)

    for x1 in (*range(NT - 2, NT), *range(NT // 2 + 2)):
        row_step(x1)
    make_group(0)
    pl.semaphore_wait(barrier, NT + 2)
    send_group(0)
    make_group(1)
    send_group(1)
    for x1 in range(NT // 2 + 2, NT - 2):
        row_step(x1)
    for g in (2, 3):
        make_group(g)
        send_group(g)
    column_copy.wait()
    gain_copy.wait()

    def wait_group(g, semaphores):
        most = pl.ds(0, NT - 1)
        pltpu.make_async_copy(
            blocks.at[most, rows_of(g)], landing.at[most, rows_of(g)], semaphores.at[g]
        ).wait()

    phase = tap_index[0, 1]
    weights = [taps[phase, tap] for tap in range(5)]
    upper = jnp.where(me < shift[0], 1.0, 0.0)
    first = jnp.full((META, CHUNK), offset[0].astype(f32))
    kind = lax.broadcasted_iota(jnp.int32, (META, CHUNK), 0)
    facts = jnp.where(kind == 0, first, upper)

    def start_image(g):
        transform_rows(landing, first_row(g), ROWS)
        for y1 in range(NT):
            high, low = split(spectrum[y1, pl.ds(0, ROWS), :])
            both = lax.dot_general(
                table[y1],
                jnp.concatenate([high, low], axis=1),
                (((1,), (1,)), ((), ())),
                preferred_element_type=f32,
            )
            padded[pl.ds(PAD + y1, SIDE, stride=NT), pl.ds(0, ROWS)] = both[:SIDE] + both[SIDE:]

    def finish_image(g):
        for part in range(G // 128):
            total = weights[0] * padded[pl.ds(part * 128 + PAD + 2, 128), :]
            for tap in range(1, 5):
                total = total + weights[tap] * padded[pl.ds(part * 128 + PAD + 2 - tap, 128), :]
            at = pl.ds(part * 128, 128)
            smooth[:, at] = total.T[:ROWS] * gain[0, rows_of(g), at]
        rolled = pltpu.roll(smooth[...], offset[0], 1)
        for chunk in range(4):
            piece = rolled[:, chunk * CHUNK : (chunk + 1) * CHUNK]
            pieces[g, chunk % 2, chunk // 2, pl.ds(0, ROWS), :] = piece
            pieces[g, chunk % 2, chunk // 2, pl.ds(ROWS, META), :] = facts

    def pair(g):
        return pltpu.make_async_remote_copy(
            src_ref=pieces.at[g, 1 - core],
            dst_ref=paired.at[g],
            send_sem=pair_send.at[g],
            recv_sem=pair_recv.at[g],
            device_id={"beam": mate},
            device_id_type=MESH,
        )

    def ring(g, number, peer):
        return pltpu.make_async_remote_copy(
            src_ref=terms.at[g, number],
            dst_ref=landed.at[g, number],
            send_sem=ring_send.at[g, number],
            recv_sem=ring_recv.at[g, number],
            device_id={"beam": peer},
            device_id_type=MESH,
        )

    lane = lax.broadcasted_iota(jnp.int32, (1, CHUNK), 1)

    def term(source, half, which):
        part, late = lax.rem(half, 2), half // 2
        row = (lane + CHUNK * (2 * part + core)).astype(f32)
        told = source[part, pl.ds(ROWS, META), :]
        is_late = jnp.where(row < told[0:1], 1, 0)
        here = (is_late == late) & (told[1:2] == float(which))
        return jnp.where(here, source[part, pl.ds(0, ROWS), :], 0.0)

    def both_terms(g, half, which):
        return term(pieces.at[g, core], half, which) + term(paired.at[g], half, which)

    far, above, below = lax.rem(level + 2, 4), lax.rem(level + 1, 4), lax.rem(level + 3, 4)
    peers = (up, down, up, down, up, down)

    def first_hop(g):
        pair(g).wait_recv()
        for number, half, which in ((0, far, 0), (1, far, 1), (2, above, 1), (3, below, 0)):
            terms[g, number] = both_terms(g, half, which)
            ring(g, number, peers[number]).start()
        terms[g, 4] = both_terms(g, above, 0)
        terms[g, 5] = both_terms(g, below, 1)

    def second_hop(g):
        for number in (0, 1):
            ring(g, number, peers[number]).wait_recv()
            terms[g, 4 + number] += landed[g, number]
            ring(g, 4 + number, peers[4 + number]).start()

    def group(g, carry):
        wait_group(g, tile_recv)
        start_image(g)

        @pl.when(g > 0)
        def _():
            first_hop(g - 1)

        finish_image(g)
        pair(g).start()

        return carry

    lax.fori_loop(0, GROUPS, group, 0)
    first_hop(GROUPS - 1)
    for g in range(GROUPS):
        second_hop(g)

    def finish(g, carry):
        wait_group(g, tile_send)
        pair(g).wait_send()
        for which in (0, 1):
            total = both_terms(g, level, which)
            for number in (3 - which, 4 + which):
                ring(g, number, peers[number]).wait_recv()
                total += landed[g, number]
            out[which, rows_of(g), :] = total
        for number in range(6):
            ring(g, number, peers[number]).wait_send()
        return carry

    lax.fori_loop(0, GROUPS, finish, 0)


SMEM = pl.BlockSpec(memory_space=pltpu.SMEM)
VMEM = pl.BlockSpec(memory_space=pltpu.VMEM)
ANY = pl.BlockSpec(memory_space=pl.ANY)


def gridded(model, observed, coords, count, block, cell):
    return pl.pallas_call(
        grid_kernel,
        out_shape=pltpu.VMEM((NT, SIDE, 2 * SIDE), f32),
        in_specs=[VMEM] * 3 + [SMEM] * 3,
        out_specs=VMEM,
        scratch_shapes=[
            pltpu.VMEM((NT, 2 * SIDE, 2 * SIDE), bf16),
            pltpu.VMEM((SIDE, 2 * SIDE), f32),
            pltpu.VMEM((SIDE, 2 * SIDE), f32),
        ],
        compiler_params=pltpu.CompilerParams(vmem_limit_bytes=VMEM_LIMIT),
        name="grid_residuals",
    )(model, observed, coords, count, block, cell)


def finished(grid, gain, offset, shift, tap_index, taps):
    return pl.pallas_call(
        tail_kernel,
        out_shape=pltpu.VMEM((2, SIDE, CHUNK), f32),
        in_specs=[VMEM, ANY] + [SMEM] * 4 + [ANY] * 2,
        out_specs=VMEM,
        scratch_shapes=[
            pltpu.VMEM((NT, 2 * SIDE, 3 * SIDE), bf16),
            pltpu.VMEM((NT, 2 * SIDE, 4 * SIDE), bf16),
            pltpu.VMEM((1, SIDE, G), f32),
            pltpu.VMEM((NT, ROWS, 2 * SIDE), f32),
            pltpu.VMEM((NT, SIDE, 2 * SIDE), f32),
            pltpu.VMEM((NT, SIDE, 2 * SIDE), f32),
            pltpu.VMEM((NT, SIDE, 2 * SIDE), f32),
            pltpu.VMEM((G + 2 * PAD, 2 * SIDE), f32),
            pltpu.VMEM((ROWS, G), f32),
            pltpu.VMEM((GROUPS, 2, 2, ROWS + META, CHUNK), f32),
            pltpu.VMEM((GROUPS, 2, ROWS + META, CHUNK), f32),
            pltpu.VMEM((GROUPS, 6, ROWS, CHUNK), f32),
            pltpu.VMEM((GROUPS, 6, ROWS, CHUNK), f32),
            pltpu.SemaphoreType.DMA((3,)),
            pltpu.SemaphoreType.DMA((GROUPS,)),
            pltpu.SemaphoreType.DMA((GROUPS,)),
            pltpu.SemaphoreType.DMA((GROUPS,)),
            pltpu.SemaphoreType.DMA((GROUPS,)),
            pltpu.SemaphoreType.DMA((GROUPS, 6)),
            pltpu.SemaphoreType.DMA((GROUPS, 6)),
        ],
        compiler_params=pltpu.CompilerParams(
            collective_id=0, has_side_effects=True, vmem_limit_bytes=VMEM_LIMIT
        ),
        name="image_and_sum",
    )(
        grid, gain, offset, shift, tap_index, taps,
        jnp.asarray(row_tables()), jnp.asarray(column_tables()),
    )


def local(
    model_grid, observed, coords, vis_count, subgrid_block, subgrid_cell, beam_gain,
    column_shift, row_offset, interp_index, interp_taps,
):
    grid = gridded(
        model_grid, observed, coords, vis_count, subgrid_block, subgrid_cell,
    )
    grid = pltpu.with_memory_space_constraint(grid, pltpu.VMEM)
    return finished(grid, beam_gain, row_offset, column_shift, interp_index, interp_taps)


def solution(mesh):
    placed = (
        P("beam", None, "tile", None),
        P("beam", "tile", None, None),
        P("beam", "tile", None, None),
        P("beam", "tile", None),
        P("beam", "tile", None),
        P("beam", "tile", None),
        P("beam", "tile", None),
        P("beam"),
        P("beam"),
        P("beam", None),
        P(),
    )
    return jax.shard_map(
        local, mesh=mesh, in_specs=placed, out_specs=P(None, "tile", "beam"), check_vma=False
    )
```

```python
import math

import jax
import jax.numpy as jnp
import numpy as np
from jax import lax
from jax.experimental import pallas as pl
from jax.experimental.pallas import tpu as pltpu
from jax.sharding import PartitionSpec as P

SIDE = 64
NT = 32
G = 2048
SLOTS = 256
SUBS = 64
SCALE = 3.0
PAD = 8
BEAMS = 8
CHUNK = 512
GROUPS = 4
ROWS = SIDE // GROUPS
META = 8
VMEM_LIMIT = 56 * 1024 * 1024
MESH = pl.DeviceIdType.MESH

f32 = jnp.float32
bf16 = jnp.bfloat16


def split_np(table):
    high = np.asarray(table, np.float32).astype(bf16)
    low = (np.asarray(table, np.float64) - high.astype(np.float64)).astype(np.float32).astype(bf16)
    return high, low


def row_tables():
    x1 = np.arange(NT)[:, None, None]
    x2 = np.arange(SIDE)[None, :, None]
    w = np.arange(SIDE)[None, None, :]
    angle = 2.0 * math.pi * ((w * (NT * x2 + x1)) % G) / G
    high, low = split_np(np.concatenate([np.cos(angle), np.sin(angle)], axis=1))
    return np.concatenate([high, high, low], axis=2)


def column_tables():
    y1 = np.arange(NT)[:, None, None]
    y2 = np.arange(SIDE)[None, :, None]
    r = np.arange(SIDE)[None, None, :]
    angle = 2.0 * math.pi * ((r * (NT * y2 + y1)) % G) / G
    high, low = split_np(np.concatenate([np.cos(angle), -np.sin(angle)], axis=2) / G)
    top = np.concatenate([high, high], axis=2)
    bottom = np.concatenate([low, np.zeros_like(low)], axis=2)
    return np.concatenate([top, bottom], axis=1)


def split(value):
    high = value.astype(bf16)
    low = (value - high.astype(f32)).astype(bf16)
    return high, low


def lane_signs(shape):
    lane = lax.broadcasted_iota(jnp.int32, shape, 1)
    return jnp.where(lane < SIDE, -1.0, 1.0).astype(f32)


def swapped(value):
    return pltpu.roll(value, SIDE, 1)


def transform(parts, signs):
    n = len(parts)
    if n == 1:
        return parts
    even = transform(parts[0::2], signs)
    odd = transform(parts[1::2], signs)
    low, high = [], []
    for k in range(n // 2):
        if k == 0:
            turned = odd[k]
        elif 4 * k == n:
            turned = swapped(odd[k]) * signs
        else:
            angle = 2.0 * math.pi * k / n
            turned = odd[k] * math.cos(angle) + swapped(odd[k]) * (signs * math.sin(angle))
        low.append(even[k] + turned)
        high.append(even[k] - turned)
    return low + high


def grid_kernel(
    model, observed, coords, count, block, cell, grid, windows, rising, falling
):
    row = lax.broadcasted_iota(jnp.int32, (SIDE, 2 * SIDE), 0).astype(f32)
    rising[...] = jnp.exp(row / SCALE)
    falling[...] = jnp.exp(row / -SCALE)
    left = lax.broadcasted_iota(jnp.int32, (SIDE, 2 * SIDE), 1) < SIDE

    def prepare(pair, carry):
        at = pl.ds(pl.multiple_of(pair * 2 * SIDE, 2 * SIDE), 2 * SIDE)
        for plane in range(2):
            value = model[0, plane, :, at]
            high = value.astype(bf16).astype(f32)
            low = value - high
            rows = pl.ds(plane * SIDE, SIDE)
            windows[2 * pair, rows, :] = jnp.where(left, high, swapped(low)).astype(bf16)
            windows[2 * pair + 1, rows, :] = jnp.where(left, swapped(high), low).astype(bf16)
        return carry

    lax.fori_loop(0, NT // 2, prepare, 0, unroll=8)
    grid[...] = jnp.zeros_like(grid)
    slot = lax.broadcasted_iota(jnp.int32, (2, SLOTS), 1)

    def one(i):
        k = block[0, 0, i]
        q = cell[0, 0, i]
        position = coords[0, k]
        near = jnp.exp(position / -SCALE)
        far = jnp.exp(position / SCALE)
        up = jnp.concatenate([rising[...], rising[...]], axis=1)
        down = jnp.concatenate([falling[...], falling[...]], axis=1)
        along_v = jnp.minimum(up * near[0:1], down * far[0:1])
        along_u = jnp.minimum(up * near[1:2], down * far[1:2])
        high_u, low_u = split(along_u)
        window = windows[q]
        rows = jnp.dot(
            jnp.concatenate([window, window], axis=1),
            jnp.concatenate([high_u, high_u, low_u, low_u], axis=0),
            preferred_element_type=f32,
        )
        predicted = jnp.sum(rows.reshape(2, SIDE, SLOTS) * along_v[None], axis=1)
        residual = jnp.where(slot < count[0, 0, i], observed[0, k] - predicted, 0.0)
        weighted = jnp.concatenate([along_v * residual[0:1], along_v * residual[1:2]], axis=0)
        high_w, low_w = split(weighted.T)
        products = jnp.dot(
            jnp.concatenate([high_u, low_u], axis=0),
            jnp.concatenate([high_w, low_w], axis=1),
            preferred_element_type=f32,
        )
        patch = products[:SIDE, : 2 * SIDE] + (
            products[SIDE:, : 2 * SIDE] + products[:SIDE, 2 * SIDE :]
        )
        return q, patch

    for q, patch in [one(i) for i in range(SUBS)]:
        grid[q] += patch


def tail_kernel(
    grid, gain_in, offset, shift, tap_index, taps, row_table_in, table_in, out,
    row_table, table, gain, tapped, blocks, landing, spectrum, padded, smooth,
    pieces, paired, terms, landed,
    in_sem, tile_send, tile_recv, pair_send, pair_recv, ring_send, ring_recv,
):
    me = lax.axis_index("tile")
    beam = lax.axis_index("beam")
    level, core = beam // 2, lax.rem(beam, 2)
    mate = beam + 1 - 2 * core
    up, down = lax.rem(beam + 2, BEAMS), lax.rem(beam + 6, BEAMS)
    barrier = pltpu.get_barrier_semaphore()
    for step in range(1, NT):
        pl.semaphore_signal(
            barrier, inc=1, device_id={"tile": lax.rem(me + step, NT)}, device_id_type=MESH
        )
    for peer in (mate, up, down):
        pl.semaphore_signal(barrier, inc=1, device_id={"beam": peer}, device_id_type=MESH)
    row_copy = pltpu.make_async_copy(row_table_in, row_table, in_sem.at[0])
    row_copy.start()
    column_copy = pltpu.make_async_copy(table_in, table, in_sem.at[1])
    column_copy.start()
    gain_copy = pltpu.make_async_copy(gain_in, gain, in_sem.at[2])
    gain_copy.start()

    signs = lane_signs((8, 2 * SIDE))

    def transform_rows(source, start, rows):
        def tile(i, carry):
            at = pl.ds(pl.multiple_of(start + i * 8, 8), 8)
            to = pl.ds(pl.multiple_of(i * 8, 8), 8)
            for k, value in enumerate(transform([source[t, at, :] for t in range(NT)], signs)):
                spectrum[k, to, :] = value
            return carry

        lax.fori_loop(0, rows // 8, tile, 0, unroll=4 if rows > 32 else 2)

    padded[pl.ds(0, PAD), :] = jnp.zeros((PAD, 2 * SIDE), f32)
    padded[pl.ds(PAD + G, PAD), :] = jnp.zeros((PAD, 2 * SIDE), f32)
    transform_rows(grid, 0, SIDE)
    row_copy.wait()
    wide_signs = lane_signs((SIDE, 2 * SIDE))

    def row_step(x1):
        high, low = split(spectrum[x1])
        both = jnp.dot(
            row_table[x1], jnp.concatenate([high, low, high], axis=0), preferred_element_type=f32
        )
        padded[pl.ds(PAD + x1, SIDE, stride=NT), :] = both[:SIDE] + swapped(both[SIDE:]) * wide_signs

    def first_row(g):
        return pl.multiple_of((lax.rem(g, 2) * 2 + g // 2) * ROWS, ROWS)

    def rows_of(g):
        return pl.ds(first_row(g), ROWS)

    phase_x = tap_index[0, 0]
    weights_x = [taps[phase_x, tap] for tap in range(5)]
    steps = shift[0]

    def make_group(g):
        def make(d, carry):
            start = pl.multiple_of(d * SIDE + first_row(g), ROWS)
            total = weights_x[0] * padded[pl.ds(start + PAD + 2, ROWS), :]
            for tap in range(1, 5):
                total = total + weights_x[tap] * padded[pl.ds(start + PAD + 2 - tap, ROWS), :]
            tapped[d] = total
            return carry

        def place(d, carry):
            blocks[d, rows_of(g), :] = tapped[lax.rem(d - steps + NT, NT)]
            return carry

        lax.fori_loop(0, NT, make, 0, unroll=8)
        lax.fori_loop(0, NT, place, 0, unroll=8)
        landing[me, rows_of(g), :] = blocks[me, rows_of(g), :]

    side, place_xy = me // 16, lax.rem(me, 16)

    def peer_of(step):
        return lax.rem(side + 1 + step, 2) * 16 + lax.rem(place_xy + step // 2, 16)

    def send_group(g):
        def send_one(step, inner):
            peer = peer_of(step)
            pltpu.make_async_remote_copy(
                src_ref=blocks.at[peer, rows_of(g)],
                dst_ref=landing.at[me, rows_of(g)],
                send_sem=tile_send.at[g],
                recv_sem=tile_recv.at[g],
                device_id={"tile": peer},
                device_id_type=MESH,
            ).start()
            return inner

        send_one(0, 0)
        lax.fori_loop(2, NT, send_one, 0)

    for x1 in (*range(NT - 2, NT), *range(NT // 2 + 2)):
        row_step(x1)
    make_group(0)
    pl.semaphore_wait(barrier, NT + 2)
    send_group(0)
    make_group(1)
    send_group(1)
    for x1 in range(NT // 2 + 2, NT - 2):
        row_step(x1)
    for g in (2, 3):
        make_group(g)
        send_group(g)
    column_copy.wait()
    gain_copy.wait()

    def wait_group(g, semaphores):
        most = pl.ds(0, NT - 1)
        pltpu.make_async_copy(
            blocks.at[most, rows_of(g)], landing.at[most, rows_of(g)], semaphores.at[g]
        ).wait()

    phase = tap_index[0, 1]
    weights = [taps[phase, tap] for tap in range(5)]
    upper = jnp.where(me < shift[0], 1.0, 0.0)
    first = jnp.full((META, CHUNK), offset[0].astype(f32))
    kind = lax.broadcasted_iota(jnp.int32, (META, CHUNK), 0)
    facts = jnp.where(kind == 0, first, upper)

    def column_steps(first, last):
        for y1 in range(first, last):
            high, low = split(spectrum[y1, pl.ds(0, ROWS), :])
            both = lax.dot_general(
                table[y1],
                jnp.concatenate([high, low], axis=1),
                (((1,), (1,)), ((), ())),
                preferred_element_type=f32,
            )
            padded[pl.ds(PAD + y1, SIDE, stride=NT), pl.ds(0, ROWS)] = both[:SIDE] + both[SIDE:]

    def finish_image(g):
        for part in range(G // 128):
            total = weights[0] * padded[pl.ds(part * 128 + PAD + 2, 128), :]
            for tap in range(1, 5):
                total = total + weights[tap] * padded[pl.ds(part * 128 + PAD + 2 - tap, 128), :]
            at = pl.ds(part * 128, 128)
            smooth[:, at] = total.T[:ROWS] * gain[0, rows_of(g), at]
        rolled = pltpu.roll(smooth[...], offset[0], 1)
        for chunk in range(4):
            piece = rolled[:, chunk * CHUNK : (chunk + 1) * CHUNK]
            pieces[g, chunk % 2, chunk // 2, pl.ds(0, ROWS), :] = piece
            pieces[g, chunk % 2, chunk // 2, pl.ds(ROWS, META), :] = facts

    def pair(g):
        return pltpu.make_async_remote_copy(
            src_ref=pieces.at[g, 1 - core],
            dst_ref=paired.at[g],
            send_sem=pair_send.at[g],
            recv_sem=pair_recv.at[g],
            device_id={"beam": mate},
            device_id_type=MESH,
        )

    def ring(g, number, peer):
        return pltpu.make_async_remote_copy(
            src_ref=terms.at[g, number],
            dst_ref=landed.at[g, number],
            send_sem=ring_send.at[g, number],
            recv_sem=ring_recv.at[g, number],
            device_id={"beam": peer},
            device_id_type=MESH,
        )

    lane = lax.broadcasted_iota(jnp.int32, (1, CHUNK), 1)

    def term(source, half, which):
        part, late = lax.rem(half, 2), half // 2
        row = (lane + CHUNK * (2 * part + core)).astype(f32)
        told = source[part, pl.ds(ROWS, META), :]
        is_late = jnp.where(row < told[0:1], 1, 0)
        here = (is_late == late) & (told[1:2] == float(which))
        return jnp.where(here, source[part, pl.ds(0, ROWS), :], 0.0)

    def both_terms(g, half, which):
        return term(pieces.at[g, core], half, which) + term(paired.at[g], half, which)

    far, above, below = lax.rem(level + 2, 4), lax.rem(level + 1, 4), lax.rem(level + 3, 4)
    peers = (up, down, up, down, up, down)

    def first_hop(g):
        pair(g).wait_recv()
        for number, half, which in ((0, far, 0), (1, far, 1), (2, above, 1), (3, below, 0)):
            terms[g, number] = both_terms(g, half, which)
            ring(g, number, peers[number]).start()
        terms[g, 4] = both_terms(g, above, 0)
        terms[g, 5] = both_terms(g, below, 1)

    def second_hop(g):
        for number in (0, 1):
            ring(g, number, peers[number]).wait_recv()
            terms[g, 4 + number] += landed[g, number]
            ring(g, 4 + number, peers[4 + number]).start()

    def group(g, carry):
        wait_group(g, tile_recv)
        transform_rows(landing, first_row(g), ROWS)
        column_steps(0, NT // 2)

        @pl.when(g > 0)
        def _():
            first_hop(g - 1)

        column_steps(NT // 2, NT)
        finish_image(g)
        pair(g).start()

        return carry

    lax.fori_loop(0, GROUPS, group, 0)
    first_hop(GROUPS - 1)
    for g in range(GROUPS):
        second_hop(g)

    def finish(g, carry):
        wait_group(g, tile_send)
        pair(g).wait_send()
        for which in (0, 1):
            total = both_terms(g, level, which)
            for number in (3 - which, 4 + which):
                ring(g, number, peers[number]).wait_recv()
                total += landed[g, number]
            out[which, rows_of(g), :] = total
        for number in range(6):
            ring(g, number, peers[number]).wait_send()
        return carry

    lax.fori_loop(0, GROUPS, finish, 0)


SMEM = pl.BlockSpec(memory_space=pltpu.SMEM)
VMEM = pl.BlockSpec(memory_space=pltpu.VMEM)
ANY = pl.BlockSpec(memory_space=pl.ANY)


def gridded(model, observed, coords, count, block, cell):
    return pl.pallas_call(
        grid_kernel,
        out_shape=pltpu.VMEM((NT, SIDE, 2 * SIDE), f32),
        in_specs=[VMEM] * 3 + [SMEM] * 3,
        out_specs=VMEM,
        scratch_shapes=[
            pltpu.VMEM((NT, 2 * SIDE, 2 * SIDE), bf16),
            pltpu.VMEM((SIDE, 2 * SIDE), f32),
            pltpu.VMEM((SIDE, 2 * SIDE), f32),
        ],
        compiler_params=pltpu.CompilerParams(vmem_limit_bytes=VMEM_LIMIT),
        name="grid_residuals",
    )(model, observed, coords, count, block, cell)


def finished(grid, gain, offset, shift, tap_index, taps):
    return pl.pallas_call(
        tail_kernel,
        out_shape=pltpu.VMEM((2, SIDE, CHUNK), f32),
        in_specs=[VMEM, ANY] + [SMEM] * 4 + [ANY] * 2,
        out_specs=VMEM,
        scratch_shapes=[
            pltpu.VMEM((NT, 2 * SIDE, 3 * SIDE), bf16),
            pltpu.VMEM((NT, 2 * SIDE, 4 * SIDE), bf16),
            pltpu.VMEM((1, SIDE, G), f32),
            pltpu.VMEM((NT, ROWS, 2 * SIDE), f32),
            pltpu.VMEM((NT, SIDE, 2 * SIDE), f32),
            pltpu.VMEM((NT, SIDE, 2 * SIDE), f32),
            pltpu.VMEM((NT, SIDE, 2 * SIDE), f32),
            pltpu.VMEM((G + 2 * PAD, 2 * SIDE), f32),
            pltpu.VMEM((ROWS, G), f32),
            pltpu.VMEM((GROUPS, 2, 2, ROWS + META, CHUNK), f32),
            pltpu.VMEM((GROUPS, 2, ROWS + META, CHUNK), f32),
            pltpu.VMEM((GROUPS, 6, ROWS, CHUNK), f32),
            pltpu.VMEM((GROUPS, 6, ROWS, CHUNK), f32),
            pltpu.SemaphoreType.DMA((3,)),
            pltpu.SemaphoreType.DMA((GROUPS,)),
            pltpu.SemaphoreType.DMA((GROUPS,)),
            pltpu.SemaphoreType.DMA((GROUPS,)),
            pltpu.SemaphoreType.DMA((GROUPS,)),
            pltpu.SemaphoreType.DMA((GROUPS, 6)),
            pltpu.SemaphoreType.DMA((GROUPS, 6)),
        ],
        compiler_params=pltpu.CompilerParams(
            collective_id=0, has_side_effects=True, vmem_limit_bytes=VMEM_LIMIT
        ),
        name="image_and_sum",
    )(
        grid, gain, offset, shift, tap_index, taps,
        jnp.asarray(row_tables()), jnp.asarray(column_tables()),
    )


def local(
    model_grid, observed, coords, vis_count, subgrid_block, subgrid_cell, beam_gain,
    column_shift, row_offset, interp_index, interp_taps,
):
    grid = gridded(
        model_grid, observed, coords, vis_count, subgrid_block, subgrid_cell,
    )
    grid = pltpu.with_memory_space_constraint(grid, pltpu.VMEM)
    return finished(grid, beam_gain, row_offset, column_shift, interp_index, interp_taps)


def solution(mesh):
    placed = (
        P("beam", None, "tile", None),
        P("beam", "tile", None, None),
        P("beam", "tile", None, None),
        P("beam", "tile", None),
        P("beam", "tile", None),
        P("beam", "tile", None),
        P("beam", "tile", None),
        P("beam"),
        P("beam"),
        P("beam", None),
        P(),
    )
    return jax.shard_map(
        local, mesh=mesh, in_specs=placed, out_specs=P(None, "tile", "beam"), check_vma=False
    )
```

```python
import math

import jax
import jax.numpy as jnp
import numpy as np
from jax import lax
from jax.experimental import pallas as pl
from jax.experimental.pallas import tpu as pltpu
from jax.sharding import PartitionSpec as P

SIDE = 64
NT = 32
G = 2048
SLOTS = 256
SUBS = 64
SCALE = 3.0
PAD = 8
BEAMS = 8
CHUNK = 512
GROUPS = 4
ROWS = SIDE // GROUPS
META = 8
VMEM_LIMIT = 56 * 1024 * 1024
MESH = pl.DeviceIdType.MESH

f32 = jnp.float32
bf16 = jnp.bfloat16


def split_np(table):
    high = np.asarray(table, np.float32).astype(bf16)
    low = (np.asarray(table, np.float64) - high.astype(np.float64)).astype(np.float32).astype(bf16)
    return high, low


def row_tables():
    x1 = np.arange(NT)[:, None, None]
    x2 = np.arange(SIDE)[None, :, None]
    w = np.arange(SIDE)[None, None, :]
    angle = 2.0 * math.pi * ((w * (NT * x2 + x1)) % G) / G
    high, low = split_np(np.concatenate([np.cos(angle), np.sin(angle)], axis=1))
    return np.concatenate([high, high, low], axis=2)


def column_tables():
    y1 = np.arange(NT)[:, None, None]
    y2 = np.arange(SIDE)[None, :, None]
    r = np.arange(SIDE)[None, None, :]
    angle = 2.0 * math.pi * ((r * (NT * y2 + y1)) % G) / G
    high, low = split_np(np.concatenate([np.cos(angle), -np.sin(angle)], axis=2) / G)
    top = np.concatenate([high, high], axis=2)
    bottom = np.concatenate([low, np.zeros_like(low)], axis=2)
    return np.concatenate([top, bottom], axis=1)


def split(value):
    high = value.astype(bf16)
    low = (value - high.astype(f32)).astype(bf16)
    return high, low


def lane_signs(shape):
    lane = lax.broadcasted_iota(jnp.int32, shape, 1)
    return jnp.where(lane < SIDE, -1.0, 1.0).astype(f32)


def swapped(value):
    return pltpu.roll(value, SIDE, 1)


def transform(parts, signs):
    n = len(parts)
    if n == 1:
        return parts
    even = transform(parts[0::2], signs)
    odd = transform(parts[1::2], signs)
    low, high = [], []
    for k in range(n // 2):
        if k == 0:
            turned = odd[k]
        elif 4 * k == n:
            turned = swapped(odd[k]) * signs
        else:
            angle = 2.0 * math.pi * k / n
            turned = odd[k] * math.cos(angle) + swapped(odd[k]) * (signs * math.sin(angle))
        low.append(even[k] + turned)
        high.append(even[k] - turned)
    return low + high


def grid_kernel(
    model, observed, coords, count, block, cell, grid, windows, rising, falling
):
    row = lax.broadcasted_iota(jnp.int32, (SIDE, 2 * SIDE), 0).astype(f32)
    rising[...] = jnp.exp(row / SCALE)
    falling[...] = jnp.exp(row / -SCALE)
    left = lax.broadcasted_iota(jnp.int32, (SIDE, 2 * SIDE), 1) < SIDE

    def prepare(pair, carry):
        at = pl.ds(pl.multiple_of(pair * 2 * SIDE, 2 * SIDE), 2 * SIDE)
        for plane in range(2):
            value = model[0, plane, :, at]
            high = value.astype(bf16).astype(f32)
            low = value - high
            rows = pl.ds(plane * SIDE, SIDE)
            windows[2 * pair, rows, :] = jnp.where(left, high, swapped(low)).astype(bf16)
            windows[2 * pair + 1, rows, :] = jnp.where(left, swapped(high), low).astype(bf16)
        return carry

    lax.fori_loop(0, NT // 2, prepare, 0, unroll=8)
    grid[...] = jnp.zeros_like(grid)
    slot = lax.broadcasted_iota(jnp.int32, (2, SLOTS), 1)

    def one(i):
        k = block[0, 0, i]
        q = cell[0, 0, i]
        position = coords[0, k]
        near = jnp.exp(position / -SCALE)
        far = jnp.exp(position / SCALE)
        up = jnp.concatenate([rising[...], rising[...]], axis=1)
        down = jnp.concatenate([falling[...], falling[...]], axis=1)
        along_v = jnp.minimum(up * near[0:1], down * far[0:1])
        along_u = jnp.minimum(up * near[1:2], down * far[1:2])
        high_u, low_u = split(along_u)
        window = windows[q]
        rows = jnp.dot(
            jnp.concatenate([window, window], axis=1),
            jnp.concatenate([high_u, high_u, low_u, low_u], axis=0),
            preferred_element_type=f32,
        )
        predicted = jnp.sum(rows.reshape(2, SIDE, SLOTS) * along_v[None], axis=1)
        residual = jnp.where(slot < count[0, 0, i], observed[0, k] - predicted, 0.0)
        weighted = jnp.concatenate([along_v * residual[0:1], along_v * residual[1:2]], axis=0)
        high_w, low_w = split(weighted.T)
        products = jnp.dot(
            jnp.concatenate([high_u, low_u], axis=0),
            jnp.concatenate([high_w, low_w], axis=1),
            preferred_element_type=f32,
        )
        patch = products[:SIDE, : 2 * SIDE] + (
            products[SIDE:, : 2 * SIDE] + products[:SIDE, 2 * SIDE :]
        )
        return q, patch

    for q, patch in [one(i) for i in range(SUBS)]:
        grid[q] += patch


def tail_kernel(
    grid, gain_in, offset, shift, tap_index, taps, row_table_in, table_in, out,
    row_table, table, gain, tapped, blocks, landing, spectrum, padded, smooth,
    pieces, paired, terms, landed,
    in_sem, tile_send, tile_recv, pair_send, pair_recv, ring_send, ring_recv,
):
    me = lax.axis_index("tile")
    beam = lax.axis_index("beam")
    level, core = beam // 2, lax.rem(beam, 2)
    mate = beam + 1 - 2 * core
    up, down = lax.rem(beam + 2, BEAMS), lax.rem(beam + 6, BEAMS)
    row_copy = pltpu.make_async_copy(row_table_in, row_table, in_sem.at[0])
    row_copy.start()
    barrier = pltpu.get_barrier_semaphore()
    for step in range(1, NT):
        pl.semaphore_signal(
            barrier, inc=1, device_id={"tile": lax.rem(me + step, NT)}, device_id_type=MESH
        )
    for peer in (mate, up, down):
        pl.semaphore_signal(barrier, inc=1, device_id={"beam": peer}, device_id_type=MESH)
    signs = lane_signs((8, 2 * SIDE))

    def transform_rows(source, start, rows):
        def tile(i, carry):
            at = pl.ds(pl.multiple_of(start + i * 8, 8), 8)
            to = pl.ds(pl.multiple_of(i * 8, 8), 8)
            for k, value in enumerate(transform([source[t, at, :] for t in range(NT)], signs)):
                spectrum[k, to, :] = value
            return carry

        lax.fori_loop(0, rows // 8, tile, 0, unroll=4 if rows > 32 else 2)

    padded[pl.ds(0, PAD), :] = jnp.zeros((PAD, 2 * SIDE), f32)
    padded[pl.ds(PAD + G, PAD), :] = jnp.zeros((PAD, 2 * SIDE), f32)
    transform_rows(grid, 0, SIDE)
    row_copy.wait()
    column_copy = pltpu.make_async_copy(table_in, table, in_sem.at[1])
    column_copy.start()
    gain_copy = pltpu.make_async_copy(gain_in, gain, in_sem.at[2])
    gain_copy.start()
    wide_signs = lane_signs((SIDE, 2 * SIDE))

    def row_step(x1):
        high, low = split(spectrum[x1])
        both = jnp.dot(
            row_table[x1], jnp.concatenate([high, low, high], axis=0), preferred_element_type=f32
        )
        padded[pl.ds(PAD + x1, SIDE, stride=NT), :] = both[:SIDE] + swapped(both[SIDE:]) * wide_signs

    def first_row(g):
        return pl.multiple_of((lax.rem(g, 2) * 2 + g // 2) * ROWS, ROWS)

    def rows_of(g):
        return pl.ds(first_row(g), ROWS)

    phase_x = tap_index[0, 0]
    weights_x = [taps[phase_x, tap] for tap in range(5)]
    steps = shift[0]

    def make_group(g):
        def make(d, carry):
            start = pl.multiple_of(d * SIDE + first_row(g), ROWS)
            total = weights_x[0] * padded[pl.ds(start + PAD + 2, ROWS), :]
            for tap in range(1, 5):
                total = total + weights_x[tap] * padded[pl.ds(start + PAD + 2 - tap, ROWS), :]
            tapped[d] = total
            return carry

        def place(d, carry):
            blocks[d, rows_of(g), :] = tapped[lax.rem(d - steps + NT, NT)]
            return carry

        lax.fori_loop(0, NT, make, 0, unroll=16)
        lax.fori_loop(0, NT, place, 0, unroll=16)
        landing[me, rows_of(g), :] = blocks[me, rows_of(g), :]

    side, place_xy = me // 16, lax.rem(me, 16)

    def peer_of(step):
        return lax.rem(side + 1 + step, 2) * 16 + lax.rem(place_xy + step // 2, 16)

    def send_group(g):
        def send_one(step, inner):
            peer = peer_of(step)
            pltpu.make_async_remote_copy(
                src_ref=blocks.at[peer, rows_of(g)],
                dst_ref=landing.at[me, rows_of(g)],
                send_sem=tile_send.at[g],
                recv_sem=tile_recv.at[g],
                device_id={"tile": peer},
                device_id_type=MESH,
            ).start()
            return inner

        send_one(0, 0)
        lax.fori_loop(2, NT, send_one, 0, unroll=10)

    for x1 in (*range(NT - 2, NT), *range(NT // 2 + 2)):
        row_step(x1)
    make_group(0)
    pl.semaphore_wait(barrier, NT + 2)
    send_group(0)
    make_group(1)
    send_group(1)
    for x1 in range(NT // 2 + 2, NT - 2):
        row_step(x1)
    for g in (2, 3):
        make_group(g)
        send_group(g)
    column_copy.wait()
    gain_copy.wait()

    def wait_group(g, semaphores):
        most = pl.ds(0, NT - 1)
        pltpu.make_async_copy(
            blocks.at[most, rows_of(g)], landing.at[most, rows_of(g)], semaphores.at[g]
        ).wait()

    phase = tap_index[0, 1]
    weights = [taps[phase, tap] for tap in range(5)]
    upper = jnp.where(me < shift[0], 1.0, 0.0)
    first = jnp.full((META, CHUNK), offset[0].astype(f32))
    kind = lax.broadcasted_iota(jnp.int32, (META, CHUNK), 0)
    facts = jnp.where(kind == 0, first, upper)

    def column_steps(first, last):
        for y1 in range(first, last):
            high, low = split(spectrum[y1, pl.ds(0, ROWS), :])
            both = lax.dot_general(
                table[y1],
                jnp.concatenate([high, low], axis=1),
                (((1,), (1,)), ((), ())),
                preferred_element_type=f32,
            )
            padded[pl.ds(PAD + y1, SIDE, stride=NT), pl.ds(0, ROWS)] = both[:SIDE] + both[SIDE:]

    def finish_image(g):
        for part in range(G // 128):
            total = weights[0] * padded[pl.ds(part * 128 + PAD + 2, 128), :]
            for tap in range(1, 5):
                total = total + weights[tap] * padded[pl.ds(part * 128 + PAD + 2 - tap, 128), :]
            at = pl.ds(part * 128, 128)
            smooth[:, at] = total.T[:ROWS] * gain[0, rows_of(g), at]
        rolled = pltpu.roll(smooth[...], offset[0], 1)
        for chunk in range(4):
            piece = rolled[:, chunk * CHUNK : (chunk + 1) * CHUNK]
            pieces[g, chunk % 2, chunk // 2, pl.ds(0, ROWS), :] = piece
            pieces[g, chunk % 2, chunk // 2, pl.ds(ROWS, META), :] = facts

    def pair(g):
        return pltpu.make_async_remote_copy(
            src_ref=pieces.at[g, 1 - core],
            dst_ref=paired.at[g],
            send_sem=pair_send.at[g],
            recv_sem=pair_recv.at[g],
            device_id={"beam": mate},
            device_id_type=MESH,
        )

    def ring(g, number, peer):
        return pltpu.make_async_remote_copy(
            src_ref=terms.at[g, number],
            dst_ref=landed.at[g, number],
            send_sem=ring_send.at[g, number],
            recv_sem=ring_recv.at[g, number],
            device_id={"beam": peer},
            device_id_type=MESH,
        )

    lane = lax.broadcasted_iota(jnp.int32, (1, CHUNK), 1)

    def term(source, half, which):
        part, late = lax.rem(half, 2), half // 2
        row = (lane + CHUNK * (2 * part + core)).astype(f32)
        told = source[part, pl.ds(ROWS, META), :]
        is_late = jnp.where(row < told[0:1], 1, 0)
        here = (is_late == late) & (told[1:2] == float(which))
        return jnp.where(here, source[part, pl.ds(0, ROWS), :], 0.0)

    def both_terms(g, half, which):
        return term(pieces.at[g, core], half, which) + term(paired.at[g], half, which)

    far, above, below = lax.rem(level + 2, 4), lax.rem(level + 1, 4), lax.rem(level + 3, 4)
    peers = (up, down, up, down, up, down)

    def first_hop(g):
        pair(g).wait_recv()
        for number, half, which in ((0, far, 0), (1, far, 1), (2, above, 1), (3, below, 0)):
            terms[g, number] = both_terms(g, half, which)
            ring(g, number, peers[number]).start()
        terms[g, 4] = both_terms(g, above, 0)
        terms[g, 5] = both_terms(g, below, 1)

    def second_hop(g):
        for number in (0, 1):
            ring(g, number, peers[number]).wait_recv()
            terms[g, 4 + number] += landed[g, number]
            ring(g, 4 + number, peers[4 + number]).start()

    def group(g, carry):
        wait_group(g, tile_recv)
        transform_rows(landing, first_row(g), ROWS)
        column_steps(0, NT // 2)

        @pl.when(g > 0)
        def _():
            first_hop(g - 1)

        column_steps(NT // 2, NT)
        finish_image(g)
        pair(g).start()

        return carry

    lax.fori_loop(0, GROUPS, group, 0)
    first_hop(GROUPS - 1)
    for g in range(GROUPS):
        second_hop(g)

    def finish(g, carry):
        wait_group(g, tile_send)
        pair(g).wait_send()
        for which in (0, 1):
            total = both_terms(g, level, which)
            for number in (3 - which, 4 + which):
                ring(g, number, peers[number]).wait_recv()
                total += landed[g, number]
            out[which, rows_of(g), :] = total
        for number in range(6):
            ring(g, number, peers[number]).wait_send()
        return carry

    lax.fori_loop(0, GROUPS, finish, 0)


SMEM = pl.BlockSpec(memory_space=pltpu.SMEM)
VMEM = pl.BlockSpec(memory_space=pltpu.VMEM)
ANY = pl.BlockSpec(memory_space=pl.ANY)


def gridded(model, observed, coords, count, block, cell):
    return pl.pallas_call(
        grid_kernel,
        out_shape=pltpu.VMEM((NT, SIDE, 2 * SIDE), f32),
        in_specs=[VMEM] * 3 + [SMEM] * 3,
        out_specs=VMEM,
        scratch_shapes=[
            pltpu.VMEM((NT, 2 * SIDE, 2 * SIDE), bf16),
            pltpu.VMEM((SIDE, 2 * SIDE), f32),
            pltpu.VMEM((SIDE, 2 * SIDE), f32),
        ],
        compiler_params=pltpu.CompilerParams(vmem_limit_bytes=VMEM_LIMIT),
        name="grid_residuals",
    )(model, observed, coords, count, block, cell)


def finished(grid, gain, offset, shift, tap_index, taps):
    return pl.pallas_call(
        tail_kernel,
        out_shape=pltpu.VMEM((2, SIDE, CHUNK), f32),
        in_specs=[VMEM, ANY] + [SMEM] * 4 + [ANY] * 2,
        out_specs=VMEM,
        scratch_shapes=[
            pltpu.VMEM((NT, 2 * SIDE, 3 * SIDE), bf16),
            pltpu.VMEM((NT, 2 * SIDE, 4 * SIDE), bf16),
            pltpu.VMEM((1, SIDE, G), f32),
            pltpu.VMEM((NT, ROWS, 2 * SIDE), f32),
            pltpu.VMEM((NT, SIDE, 2 * SIDE), f32),
            pltpu.VMEM((NT, SIDE, 2 * SIDE), f32),
            pltpu.VMEM((NT, SIDE, 2 * SIDE), f32),
            pltpu.VMEM((G + 2 * PAD, 2 * SIDE), f32),
            pltpu.VMEM((ROWS, G), f32),
            pltpu.VMEM((GROUPS, 2, 2, ROWS + META, CHUNK), f32),
            pltpu.VMEM((GROUPS, 2, ROWS + META, CHUNK), f32),
            pltpu.VMEM((GROUPS, 6, ROWS, CHUNK), f32),
            pltpu.VMEM((GROUPS, 6, ROWS, CHUNK), f32),
            pltpu.SemaphoreType.DMA((3,)),
            pltpu.SemaphoreType.DMA((GROUPS,)),
            pltpu.SemaphoreType.DMA((GROUPS,)),
            pltpu.SemaphoreType.DMA((GROUPS,)),
            pltpu.SemaphoreType.DMA((GROUPS,)),
            pltpu.SemaphoreType.DMA((GROUPS, 6)),
            pltpu.SemaphoreType.DMA((GROUPS, 6)),
        ],
        compiler_params=pltpu.CompilerParams(
            collective_id=0, has_side_effects=True, vmem_limit_bytes=VMEM_LIMIT
        ),
        name="image_and_sum",
    )(
        grid, gain, offset, shift, tap_index, taps,
        jnp.asarray(row_tables()), jnp.asarray(column_tables()),
    )


def local(
    model_grid, observed, coords, vis_count, subgrid_block, subgrid_cell, beam_gain,
    column_shift, row_offset, interp_index, interp_taps,
):
    grid = gridded(
        model_grid, observed, coords, vis_count, subgrid_block, subgrid_cell,
    )
    grid = pltpu.with_memory_space_constraint(grid, pltpu.VMEM)
    return finished(grid, beam_gain, row_offset, column_shift, interp_index, interp_taps)


def solution(mesh):
    placed = (
        P("beam", None, "tile", None),
        P("beam", "tile", None, None),
        P("beam", "tile", None, None),
        P("beam", "tile", None),
        P("beam", "tile", None),
        P("beam", "tile", None),
        P("beam", "tile", None),
        P("beam"),
        P("beam"),
        P("beam", None),
        P(),
    )
    return jax.shard_map(
        local, mesh=mesh, in_specs=placed, out_specs=P(None, "tile", "beam"), check_vma=False
    )
```
